32 devices in a mesh: dp: 4 (over x, core), ctx: 8 (over z, y).
Axes of the slice: x: 2, y: 2, z: 4, core: 2. Of those that a mesh axis runs over, the one named last changes fastest.
Arguments:
- latent: bfloat16 [4, 1024, 576], P('dp', 'ctx'), may hold values from -4 to 4
- query: bfloat16 [4, 1024, 64, 576], P('dp', 'ctx'), may hold values from -24 to 24
- out_grad: bfloat16 [4, 1024, 64, 128], P('dp', 'ctx'), may hold values from -6 to 6
- value_weight: bfloat16 [512, 8192], P('ctx'), may hold values from -0.25 to 0.25
- doc_lengths: int32 [4, 8], P('dp'), may hold values from 1 to 192, 1024 in all within a row
- resumed: int32 [4, 8], P('dp'), may hold values 0 or 1
- groups: int32 [4, 1024], P('dp', 'ctx'), may hold values from 0 to 3, never falling along the last dimension, each value on 1 to 768 neighbouring positions
- reward: float32 [4, 1024], P('dp', 'ctx'), may hold values from -2 to 43.2
Outputs:
- latent_grad: float32 [4, 1024, 576], P('dp', 'ctx')
- value_weight_grad: float32 [512, 8192], P('ctx')
The draws below stay inside these ranges and needn't reach their ends.
Inputs may be any that keep to these rules, and one draw needn't show every extreme that they name: `doc_lengths`: each sequence's lengths sum to 1024. `groups`: group ids never fall along a sequence, and every id appears in every sequence.
All inputs are finite; a program needn't handle non-finite values. No bound on the sum of `resumed` on one device may be relied on, other than what follows from the above.
Results may differ from the reference program's by a relative error of at most 0.014.
Values may be sent and summed in bfloat16 or wider, within the bound.
A program may use at most 128 MiB of HBM per device.

```python
import functools
import math
import jax
import jax.numpy as jnp
import numpy as np
from jax import lax

LAT = 512
ROPE = 64
HEADS = 64
VDIM = 128
T_DEV = 128
SEQ = 1024
BATCH = 4
DOCMAX = 192
NDOC = 8
NGROUP = 4
GROUPMAX = 768
N_CTX = 8


def latent_base(key):
    return jnp.clip(jax.random.normal(key, (BATCH, SEQ, LAT + ROPE), jnp.float32), -4.0, 4.0)


def draw_latent(key, part):
    shared = latent_base(key)
    return shared.astype(jnp.bfloat16)


def draw_query(key, part):
    key = jax.random.fold_in(key, 7)
    first_key = jax.random.fold_in(key, 0)
    full_shape = (BATCH, SEQ, HEADS, LAT + ROPE)
    noise = jnp.clip(jax.random.normal(first_key, full_shape, jnp.float32), -6.0, 6.0)
    values = noise
    return values.astype(jnp.bfloat16)


def draw_reward(key, part):
    key = jax.random.fold_in(key, 5)
    position_ramp = 1.0 + 3.0 * jnp.arange(SEQ, dtype=jnp.float32) / SEQ
    values = (0.5 * jnp.clip(jax.random.normal(key, (BATCH, SEQ), jnp.float32), -4.0, 4.0) + 1.5) * position_ramp
    return values.astype(jnp.float32)


def with_ends(values, own_key, least, largest):
    place = [jax.random.randint(jax.random.fold_in(own_key, axis), (), 0, length) for axis, length in enumerate(values.shape)]
    main_axis = values.shape.index(max(values.shape))
    neighbour = place[:main_axis] + [(place[main_axis] + 1) % values.shape[main_axis]] + place[main_axis + 1:]
    return values.at[tuple(place)].set(least).at[tuple(neighbour)].set(largest)


def level_of(stream_key, shape, cuts, smallest, largest):
    factor_of = 1.0
    for position, parts in cuts:
        draws = jax.random.uniform(jax.random.fold_in(jax.random.fold_in(stream_key, 6), position), (parts,), jnp.float32, smallest / len(cuts), largest / len(cuts))
        factor_of = factor_of * jnp.repeat(jnp.exp(draws), shape[position] // parts).reshape((-1,) + (1,) * (len(shape) - 1 - position))
    return factor_of


def profile(number_of, total, limit, slope):
    portions = [(1 << 20) // math.isqrt(standing ** slope) + 1 for standing in range(2, number_of + 1)]
    rest, holding = total - limit - (number_of - 1), [1] * (number_of - 1)
    while rest > 0:
        free = [i for i in range(number_of - 1) if holding[i] < limit]
        pool, remaining = sum([portions[i] for i in free]), rest
        for i in free:
            extra = min(limit - holding[i], max(1, remaining * portions[i] // pool), rest)
            holding[i] = holding[i] + extra
            rest = rest - extra
    return np.array([limit] + holding)


def ragged_sizes(own_key, number_of, total, bound, skew):
    if number_of == 2:
        one = jax.random.randint(own_key, (), max(1, total - bound), min(bound, total - 1) + 1)
        return jnp.stack([one, total - one])
    lengths = jnp.asarray(profile(number_of, total, bound, skew), jnp.int32)
    twos = (number_of - 1) // 2
    donor, receiver = lengths[1:1 + 2 * twos:2], lengths[2:2 + 2 * twos:2]
    margin = jnp.minimum(donor - 1, bound - receiver)
    moved = jax.random.randint(jax.random.fold_in(own_key, 1), (twos,), 0, 1 << 20) % (margin + 1)
    lengths = lengths.at[1:1 + 2 * twos:2].set(donor - moved).at[2:2 + 2 * twos:2].set(receiver + moved)
    return lengths[jax.random.permutation(jax.random.fold_in(own_key, 2), number_of)]


def normal_values(stream_key, dims, deviation, bound, pieces=(), held_as=jnp.bfloat16):
    loudness = level_of(stream_key, dims, pieces, -0.22, 0.18) if pieces else 1.0
    entries = jax.random.normal(stream_key, dims, jnp.float32) * deviation * loudness
    return jnp.minimum(jnp.maximum(entries, -bound), bound).astype(held_as)


def setup_inputs(seed: int = 0) -> dict:
    arg_keys = jax.random.split(jax.random.key(seed), 9)
    latent = draw_latent(jax.random.fold_in(arg_keys[8], 71), 0)
    query = draw_query(jax.random.fold_in(arg_keys[8], 71), 0)
    out_grad = normal_values(arg_keys[2], (BATCH, SEQ, HEADS, VDIM), 1.0, 6.0, ((0, 4), (1, 8)))
    value_weight = normal_values(arg_keys[3], (LAT, HEADS * VDIM), LAT ** -0.5, 0.25, ((0, 8),))
    doc_lengths = jax.vmap(lambda own: ragged_sizes(own, NDOC, SEQ, DOCMAX, 2))(jax.random.split(arg_keys[4], BATCH)).reshape((BATCH, NDOC)).astype(jnp.int32)
    resumed = with_ends((jax.random.randint(arg_keys[5], (BATCH, NDOC), 0, 2) < 1).astype(jnp.int32), jax.random.fold_in(arg_keys[5], 1), 0, 1)
    groups = jax.vmap(lambda own: jnp.searchsorted(jnp.cumsum(ragged_sizes(own, NGROUP, SEQ, GROUPMAX, 1)), jnp.arange(SEQ), side="right"))(jax.random.split(arg_keys[6], BATCH)).reshape((BATCH, SEQ)).astype(jnp.int32)
    reward = draw_reward(jax.random.fold_in(arg_keys[8], 71), 0)
    return {"latent": latent, "query": query, "out_grad": out_grad, "value_weight": value_weight, "doc_lengths": doc_lengths, "resumed": resumed, "groups": groups, "reward": reward}


score_scale = 192.0 ** -0.5


def block_terms(key_rows, queries, grad_block, weight_full, visible):
    head_count = queries.shape[1]
    value_dim = grad_block.shape[2]
    query_f = queries.astype(jnp.float32)
    key_f = key_rows.astype(jnp.float32)
    score = jnp.einsum("thc,kc->thk", query_f, key_f) * score_scale
    score = jnp.where(visible[:, None, :], score, -jnp.inf)
    row_peak = jnp.max(score, axis=2, keepdims=True)
    exponent = jnp.exp(score - row_peak)
    prob_full = exponent / jnp.sum(exponent, axis=2, keepdims=True)
    prob_b = prob_full.astype(jnp.bfloat16)
    values = key_f[:, :LAT]
    attended = jnp.einsum("thk,kc->thc", prob_b.astype(jnp.float32), values)
    attended_b = attended.astype(jnp.bfloat16)
    weight_f = weight_full.astype(jnp.float32).reshape(LAT, head_count, value_dim)
    grad_f = grad_block.astype(jnp.float32)
    latent_out = jnp.einsum("thv,ihv->thi", grad_f, weight_f).astype(jnp.bfloat16)
    latent_out_f = latent_out.astype(jnp.float32)
    prob_grad = jnp.einsum("thi,ki->thk", latent_out_f, values)
    row_dot = jnp.sum(latent_out_f * attended, axis=2)
    score_grad = (score_scale * prob_full * (prob_grad - row_dot[:, :, None])).astype(jnp.bfloat16)
    key_part = jnp.einsum("thk,thc->kc", score_grad.astype(jnp.float32), query_f)
    value_part = jnp.einsum("thk,thi->ki", prob_b.astype(jnp.float32), latent_out_f)
    key_term = (key_part + jnp.pad(value_part, ((0, 0), (0, ROPE)))).astype(jnp.bfloat16)
    weight_term = jnp.einsum("thi,thv->ihv", attended_b.astype(jnp.float32), grad_f)
    weight_term = weight_term.reshape(LAT, head_count * value_dim).astype(jnp.bfloat16)
    return key_term, weight_term


def span_terms(panels_back, key_rows, queries, grad_block, weight_full, visible):
    first_row = (3 - panels_back) * T_DEV
    key_term, weight_term = block_terms(key_rows[first_row:], queries, grad_block, weight_full, visible[:, first_row:])
    filler = jnp.zeros((first_row, LAT + ROPE), key_term.dtype)
    return jnp.concatenate([filler, key_term], axis=0), weight_term


def reference(latent, query, out_grad, value_weight, doc_lengths, resumed, groups, reward):
    group_count = NGROUP
    row_count = T_DEV
    latent_width = LAT + ROPE
    labels = jnp.arange(group_count, dtype=jnp.int32)
    onehot = (groups[:, :, None] == labels[None, None, :]).astype(jnp.float32)
    group_sums = jnp.sum(onehot * reward[:, :, None], axis=1)
    counts = jnp.sum(onehot, axis=1)
    group_means = group_sums / counts
    token_weight = 0.125 * (reward - jnp.sum(onehot * group_means[:, None, :], axis=2))
    scaled = (token_weight[:, :, None, None] * out_grad.astype(jnp.float32)).astype(jnp.bfloat16)
    starts = jnp.cumsum(doc_lengths, axis=1) - doc_lengths
    positions = jnp.arange(SEQ, dtype=jnp.int32)
    doc = jnp.sum((starts[:, None, :] <= positions[None, :, None]).astype(jnp.int32), axis=2) - 1
    doc_slots = jnp.arange(doc_lengths.shape[1], dtype=jnp.int32)
    resumed_at = jnp.sum(jnp.where(doc[:, :, None] == doc_slots[None, None, :], resumed[:, None, :], 0), axis=2)
    lat_pad = jnp.concatenate([jnp.zeros((BATCH, 3 * row_count, latent_width), latent.dtype), latent], axis=1)
    doc_pad = jnp.concatenate([jnp.full((BATCH, 3 * row_count), -1, jnp.int32), doc.astype(jnp.int32)], axis=1)
    anchor = jnp.zeros((), jnp.int32)
    slot_weights = jnp.array([3, 2, 1, 0], jnp.int32)
    branches = [functools.partial(span_terms, panels_back) for panels_back in range(4)]

    def block_step(running, flat_index):
        key_grads, weight_acc = running
        batch_index = (flat_index // N_CTX).astype(jnp.int32)
        block_index = (flat_index % N_CTX).astype(jnp.int32)
        offset = (block_index * row_count).astype(jnp.int32)
        key_rows = lax.dynamic_slice_in_dim(lat_pad[batch_index], offset, 4 * row_count, 0)
        key_doc = lax.dynamic_slice_in_dim(doc_pad[batch_index], offset, 4 * row_count, 0)
        query_doc = lax.dynamic_slice_in_dim(doc[batch_index], offset, row_count, 0)
        query_resumed = lax.dynamic_slice_in_dim(resumed_at[batch_index], offset, row_count, 0)
        queries = lax.dynamic_slice_in_dim(query[batch_index], offset, row_count, 0)
        grad_block = lax.dynamic_slice_in_dim(scaled[batch_index], offset, row_count, 0)
        key_pos = offset - 3 * row_count + jnp.arange(4 * row_count, dtype=jnp.int32)
        query_pos = offset + jnp.arange(row_count, dtype=jnp.int32)
        same_doc = key_doc[None, :] == query_doc[:, None]
        prior_doc = (query_resumed[:, None] == 1) & (key_doc[None, :] == query_doc[:, None] - 1)
        visible = (key_pos[None, :] <= query_pos[:, None]) & (key_pos[None, :] >= 0) & (same_doc | prior_doc)
        slot_any = jnp.any(visible.reshape(row_count, 4, row_count), axis=(0, 2)).astype(jnp.int32)
        reach_index = jnp.max(slot_weights * slot_any).astype(jnp.int32)
        key_term, weight_term = lax.switch(reach_index, branches, key_rows, queries, grad_block, value_weight, visible)
        current = lax.dynamic_slice(key_grads, (batch_index, offset, anchor), (1, 4 * row_count, latent_width))
        key_grads = lax.dynamic_update_slice(key_grads, current + key_term.astype(jnp.float32)[None], (batch_index, offset, anchor))
        weight_acc = weight_acc + weight_term.astype(jnp.float32)
        return (key_grads, weight_acc), None

    start_grads = jnp.zeros((BATCH, SEQ + 3 * row_count, latent_width), jnp.float32)
    start_weight = jnp.zeros((LAT, HEADS * VDIM), jnp.float32)
    (key_grads, weight_acc), unused = lax.scan(block_step, (start_grads, start_weight), jnp.arange(BATCH * N_CTX, dtype=jnp.int32))
    return key_grads[:, 3 * row_count:], weight_acc
```

```python
import functools

import jax
import jax.numpy as jnp
from jax import lax
from jax.experimental import pallas as pl
from jax.experimental.pallas import tpu as pltpu
from jax.sharding import PartitionSpec as P

LAT = 512
ROPE = 64
NGROUP = 4
HB = 4
BACK = 3
MESH = pl.DeviceIdType.MESH
VMEM = pltpu.VMEM

score_scale = 192.0 ** (-0.5)
LOG2E = 1.4426950408889634


def enter(targets):
    barrier = pltpu.get_barrier_semaphore()
    for target in targets:
        pl.semaphore_signal(barrier, inc=1, device_id=target, device_id_type=MESH)
    pl.semaphore_wait(barrier, len(targets))


def start_kernel(n, docs, lengths, resumed, latent, groups, reward, keys, bias, weight,
                 mine, got, key_send, key_recv, sum_send, sum_recv):
    me = lax.axis_index("ctx")
    rows = latent.shape[0]
    ids = groups[...]
    gains = reward[...]
    for g in range(NGROUP):
        hit = ids == g
        mine[g : g + 1, :] = jnp.where(hit, gains, 0.0)
        mine[NGROUP + g : NGROUP + g + 1, :] = jnp.where(hit, 1.0, 0.0)
    enter([{"ctx": lax.rem(me + d, n)} for d in range(1, n)])
    sends = []
    for d in range(1, n):
        target = {"ctx": lax.rem(me + d, n)}
        sends.append(pltpu.make_async_remote_copy(
            src_ref=mine, dst_ref=got.at[d - 1], send_sem=sum_send.at[d - 1],
            recv_sem=sum_recv.at[d - 1], device_id=target, device_id_type=MESH))
        sends[-1].start()
    moves = []
    for d in range(1, BACK + 1):
        target = {"ctx": lax.rem(me + d, n)}
        moves.append(pltpu.make_async_remote_copy(
            src_ref=latent, dst_ref=keys.at[pl.ds((BACK - d) * rows, rows)],
            send_sem=key_send.at[d - 1], recv_sem=key_recv.at[d - 1],
            device_id=target, device_id_type=MESH))
        moves[-1].start()
    keys[BACK * rows :, :] = latent[...]
    first = me * rows
    query_pos = first + lax.broadcasted_iota(jnp.int32, (1, rows), 1)
    low = jnp.zeros((1, rows), jnp.int32)
    start = jnp.int32(0)
    before = jnp.int32(0)
    for e in range(docs):
        reach = jnp.where(resumed[0, e] == 1, before, start)
        low = jnp.where(query_pos >= start, reach, low)
        before = start
        start = start + lengths[0, e]
    span = (BACK + 1) * rows
    key_pos = first - BACK * rows + lax.broadcasted_iota(jnp.int32, (span, rows), 0)
    seen = (key_pos >= low) & (key_pos <= query_pos)
    bias[...] = jnp.where(seen, 0.0, -jnp.inf)
    for copy in sends:
        copy.wait()
    total = mine[...]
    for d in range(n - 1):
        total = total + got[d]
    sums = jnp.sum(total, axis=1, keepdims=True)
    mean = jnp.zeros((1, rows), jnp.float32)
    for g in range(NGROUP):
        mean = jnp.where(ids == g, sums[g : g + 1] / sums[NGROUP + g : NGROUP + g + 1], mean)
    token = 0.125 * (gains - mean)
    weight[...] = jnp.transpose(jnp.broadcast_to(token, (rows, rows)))
    for copy in moves:
        copy.wait()


def start_call(n, lengths, resumed, latent, groups, reward):
    rows, width = latent.shape
    span = (BACK + 1) * rows
    vm = pl.BlockSpec(memory_space=VMEM)
    sm = pl.BlockSpec(memory_space=pltpu.SMEM)
    return pl.pallas_call(
        functools.partial(start_kernel, n, lengths.shape[1]),
        out_shape=(
            jax.ShapeDtypeStruct((span, width), jnp.bfloat16),
            jax.ShapeDtypeStruct((span, rows), jnp.float32),
            jax.ShapeDtypeStruct((rows, rows), jnp.float32),
        ),
        in_specs=[sm, sm, vm, vm, vm],
        out_specs=(vm, vm, vm),
        scratch_shapes=[
            VMEM((2 * NGROUP, rows), jnp.float32),
            VMEM((n - 1, 2 * NGROUP, rows), jnp.float32),
            pltpu.SemaphoreType.DMA((BACK,)),
            pltpu.SemaphoreType.DMA((BACK,)),
            pltpu.SemaphoreType.DMA((n - 1,)),
            pltpu.SemaphoreType.DMA((n - 1,)),
        ],
        compiler_params=pltpu.CompilerParams(
            collective_id=0, has_side_effects=True, vmem_limit_bytes=16 << 20),
        cost_estimate=pl.CostEstimate(flops=1 << 20, bytes_accessed=2 << 20, transcendentals=0),
    )(lengths, resumed, latent, groups, reward)


def nt(a, b):
    return lax.dot_general(a, b, (((1,), (1,)), ((), ())), preferred_element_type=jnp.float32)


def nn(a, b):
    return jnp.dot(a, b, preferred_element_type=jnp.float32)


def forward_kernel(with_sum, off, query, grad, keys, values_t, bias, weight, *rest):
    if with_sum:
        partner, prob_ref, term_ref = rest
    else:
        prob_ref, term_ref = rest
    rows = query.shape[1]
    q = query[...].reshape(HB * rows, query.shape[2])
    score = nt(keys[...], q) * (score_scale * LOG2E) + jnp.concatenate([bias[...]] * HB, axis=1)
    peak = jnp.max(score, axis=0, keepdims=True)
    exponent = jnp.exp2(score - peak)
    prob = (exponent * (1.0 / jnp.sum(exponent, axis=0, keepdims=True))).astype(jnp.bfloat16)
    prob_ref[...] = prob
    attended = nn(values_t[...], prob).astype(jnp.bfloat16)
    vdim = grad.shape[2]
    for h in range(HB):
        scaled = (weight[...] * grad[h].astype(jnp.float32)).astype(jnp.bfloat16)
        term = nn(attended[:, h * rows : (h + 1) * rows], scaled)
        part = slice(h * vdim, (h + 1) * vdim)
        if with_sum:
            term = term + partner[:, part].astype(jnp.float32)
        term_ref[:, part] = term.astype(jnp.bfloat16)


def forward_call(off, heads, query, grad, keys, values_t, bias, weight, partner=None):
    rows, width = query.shape[1:]
    vdim = grad.shape[2]
    span = keys.shape[0]
    whole = lambda shape: pl.BlockSpec(shape, lambda i, o: (0, 0))
    by_head = lambda shape: pl.BlockSpec(shape, lambda i, o: (o[0] + i, 0, 0))
    column = lambda height, wide: pl.BlockSpec((height, wide), lambda i, o: (0, i))
    in_specs = [
        by_head((HB, rows, width)), by_head((HB, rows, vdim)), whole((span, width)),
        whole((LAT, span)), whole((span, rows)), whole((rows, rows)),
    ]
    args = [query, grad, keys, values_t, bias, weight]
    if partner is not None:
        in_specs.append(column(LAT, HB * vdim))
        args.append(partner)
    flops = 2 * heads * rows * (span * (width + LAT) + LAT * vdim)
    return pl.pallas_call(
        functools.partial(forward_kernel, partner is not None),
        grid_spec=pltpu.PrefetchScalarGridSpec(
            num_scalar_prefetch=1,
            grid=(heads // HB,),
            in_specs=in_specs,
            out_specs=[column(span, HB * rows), column(LAT, HB * vdim)],
        ),
        out_shape=[
            jax.ShapeDtypeStruct((span, heads * rows), jnp.bfloat16),
            jax.ShapeDtypeStruct((LAT, heads * vdim), jnp.bfloat16),
        ],
        compiler_params=pltpu.CompilerParams(vmem_limit_bytes=48 << 20),
        cost_estimate=pl.CostEstimate(
            flops=flops, bytes_accessed=heads * rows * 4 * (width + span), transcendentals=0),
    )(off, *args)


def backward_kernel(off, query, grad, value_weight, prob_ref, keys, weight, out):
    rows = query.shape[1]
    vdim = grad.shape[2]
    q = query[...].reshape(HB * rows, query.shape[2])
    parts = []
    for h in range(HB):
        scaled = (weight[...] * grad[h].astype(jnp.float32)).astype(jnp.bfloat16)
        parts.append(nt(scaled, value_weight[:, h * vdim : (h + 1) * vdim]).astype(jnp.bfloat16))
    latent_out = jnp.concatenate(parts, axis=0)
    prob_b = prob_ref[...]
    prob = prob_b.astype(jnp.float32)
    prob_grad = nt(keys[:, :LAT], latent_out)
    row_dot = jnp.sum(prob * prob_grad, axis=0, keepdims=True)
    score_grad = (score_scale * prob * (prob_grad - row_dot)).astype(jnp.bfloat16)
    key_part = nn(score_grad, q)
    value_part = nn(prob_b, latent_out)

    @pl.when(pl.program_id(0) == 0)
    def _():
        out[...] = jnp.zeros_like(out)

    out[:, :LAT] += key_part[:, :LAT] + value_part
    out[:, LAT:] += key_part[:, LAT:]


def backward_call(off, heads, query, grad, value_weight, prob, keys, weight):
    rows, width = query.shape[1:]
    vdim = grad.shape[2]
    span = keys.shape[0]
    whole = lambda shape: pl.BlockSpec(shape, lambda i, o: (0, 0))
    by_head = lambda shape: pl.BlockSpec(shape, lambda i, o: (o[0] + i, 0, 0))
    column = lambda height, wide: pl.BlockSpec((height, wide), lambda i, o: (0, i))
    flops = 2 * heads * rows * (span * (width + 2 * LAT) + LAT * vdim)
    return pl.pallas_call(
        backward_kernel,
        grid_spec=pltpu.PrefetchScalarGridSpec(
            num_scalar_prefetch=1,
            grid=(heads // HB,),
            in_specs=[
                by_head((HB, rows, width)), by_head((HB, rows, vdim)), column(LAT, HB * vdim),
                column(span, HB * rows), whole((span, width)), whole((rows, rows)),
            ],
            out_specs=whole((span, width)),
        ),
        out_shape=jax.ShapeDtypeStruct((span, width), jnp.float32),
        compiler_params=pltpu.CompilerParams(vmem_limit_bytes=48 << 20),
        cost_estimate=pl.CostEstimate(
            flops=flops, bytes_accessed=heads * rows * 4 * (width + span), transcendentals=0),
    )(off, query, grad, value_weight, prob, keys, weight)


def key_kernel(n, first, second, out, term, got, send, recv):
    me = lax.axis_index("ctx")
    rows = out.shape[0]
    term[...] = (first[...] + second[...]).astype(jnp.bfloat16)
    enter([{"ctx": lax.rem(me + d, n)} for d in range(1, BACK + 1)]
          + [{"ctx": lax.rem(me + n - d, n)} for d in range(1, BACK + 1)])
    moves = []
    for d in range(1, BACK + 1):
        moves.append(pltpu.make_async_remote_copy(
            src_ref=term.at[pl.ds((BACK - d) * rows, rows)], dst_ref=got.at[d - 1],
            send_sem=send.at[d - 1], recv_sem=recv.at[d - 1],
            device_id={"ctx": lax.rem(me + n - d, n)}, device_id_type=MESH))
        moves[-1].start()
    total = term[BACK * rows :, :].astype(jnp.float32)
    for d in range(1, BACK + 1):
        moves[d - 1].wait()
        total = total + jnp.where(me + d < n, got[d - 1].astype(jnp.float32), 0.0)
    out[...] = total


def key_call(n, first, second):
    span, width = first.shape
    rows = span // (BACK + 1)
    vm = pl.BlockSpec(memory_space=VMEM)
    return pl.pallas_call(
        functools.partial(key_kernel, n),
        out_shape=jax.ShapeDtypeStruct((rows, width), jnp.float32),
        in_specs=[vm, vm],
        out_specs=vm,
        scratch_shapes=[
            VMEM((span, width), jnp.bfloat16),
            VMEM((BACK, rows, width), jnp.bfloat16),
            pltpu.SemaphoreType.DMA((BACK,)),
            pltpu.SemaphoreType.DMA((BACK,)),
        ],
        compiler_params=pltpu.CompilerParams(
            collective_id=1, has_side_effects=True, vmem_limit_bytes=24 << 20),
        cost_estimate=pl.CostEstimate(flops=1 << 20, bytes_accessed=3 << 20, transcendentals=0),
    )(first, second)


def finish_kernel(m, count, *refs):
    parts, (out, across, mine, other, x_send, x_recv, c_send, c_recv) = refs[:count], refs[count:]
    me = lax.axis_index("dp")
    core = lax.rem(me, 2)
    chip = me // 2
    chips = m // 2
    wide = parts[0].shape[1]
    half = wide * count
    partner = {"dp": chip * 2 + (1 - core)}
    peers = [{"dp": lax.rem(chip + d, chips) * 2 + core} for d in range(1, chips)]
    enter(peers + [partner])
    moves = []
    for j in range(count):
        row = []
        for d in range(1, chips):
            row.append(pltpu.make_async_remote_copy(
                src_ref=parts[j], dst_ref=across.at[j, chip],
                send_sem=x_send.at[j, d - 1], recv_sem=x_recv.at[j, d - 1],
                device_id=peers[d - 1], device_id_type=MESH))
            row[-1].start()
        moves.append(row)
    swaps = []
    for j in range(count):
        across[j, chip] = parts[j][...]
        for copy in moves[j]:
            copy.wait()
        total = across[j, 0].astype(jnp.float32)
        for k in range(1, chips):
            total = total + across[j, k].astype(jnp.float32)
        rounded = total.astype(jnp.bfloat16)
        mine[j] = rounded
        swaps.append(pltpu.make_async_remote_copy(
            src_ref=mine.at[j], dst_ref=other.at[j], send_sem=c_send.at[j],
            recv_sem=c_recv.at[j], device_id=partner, device_id_type=MESH))
        swaps[-1].start()
        out[:, pl.ds(pl.multiple_of(core * half + j * wide, 128), wide)] = rounded.astype(jnp.float32)
    for j in range(count):
        swaps[j].wait()
        out[:, pl.ds(pl.multiple_of((1 - core) * half + j * wide, 128), wide)] = (
            other[j].astype(jnp.float32))


def finish_call(m, parts):
    count = len(parts)
    rows, wide = parts[0].shape
    vm = pl.BlockSpec(memory_space=VMEM)
    chips = m // 2
    return pl.pallas_call(
        functools.partial(finish_kernel, m, count),
        out_shape=jax.ShapeDtypeStruct((rows, 2 * wide * count), jnp.float32),
        in_specs=[vm] * count,
        out_specs=vm,
        scratch_shapes=[
            VMEM((count, chips, rows, wide), jnp.bfloat16),
            VMEM((count, rows, wide), jnp.bfloat16),
            VMEM((count, rows, wide), jnp.bfloat16),
            pltpu.SemaphoreType.DMA((count, chips - 1)),
            pltpu.SemaphoreType.DMA((count, chips - 1)),
            pltpu.SemaphoreType.DMA((count,)),
            pltpu.SemaphoreType.DMA((count,)),
        ],
        compiler_params=pltpu.CompilerParams(
            collective_id=2, has_side_effects=True, vmem_limit_bytes=24 << 20),
        cost_estimate=pl.CostEstimate(flops=1 << 20, bytes_accessed=6 << 20, transcendentals=0),
    )(*parts)


CHUNKS = 2


def per_device(latent, query, out_grad, value_weight, doc_lengths, resumed, groups, reward):
    n = lax.axis_size("ctx")
    m = lax.axis_size("dp")
    core = lax.rem(lax.axis_index("dp"), 2)
    heads = query.shape[2]
    half = heads // 2
    quarter = half // CHUNKS
    vdim = out_grad.shape[3]
    swap = [(i, i ^ 1) for i in range(m)]
    half_rows = lax.dynamic_slice_in_dim(value_weight, core * half * vdim, half * vdim, 1)
    own_weight = lax.all_gather(half_rows, "ctx", axis=0, tiled=True)
    keys, bias, weight = start_call(n, doc_lengths, resumed, latent[0], groups, reward)
    values_t = keys[:, :LAT].T
    q = jnp.transpose(query[0], (1, 0, 2))
    grad = jnp.transpose(out_grad[0], (1, 0, 2))
    own_at = [((core * half + j * quarter) // HB).astype(jnp.int32).reshape(1) for j in range(CHUNKS)]
    other_at = [(((1 - core) * half + j * quarter) // HB).astype(jnp.int32).reshape(1)
                for j in range(CHUNKS)]
    other_prob, own_prob, arrived, sums = [], [], [], []
    for j in range(CHUNKS):
        prob, term = forward_call(other_at[j], quarter, q, grad, keys, values_t, bias, weight)
        other_prob.append(prob)
        arrived.append(lax.ppermute(term, "dp", swap))
    for j in range(CHUNKS):
        prob, term = forward_call(
            own_at[j], quarter, q, grad, keys, values_t, bias, weight, arrived[j])
        own_prob.append(prob)
        sums.append(lax.psum_scatter(term, "ctx", scatter_dimension=0, tiled=True))
    other_weight = lax.ppermute(own_weight, "dp", swap)
    pieces = []
    for at, weights, probs in ((own_at, own_weight, own_prob), (other_at, other_weight, other_prob)):
        for j in range(CHUNKS):
            pieces.append(backward_call(
                at[j], quarter, q, grad, weights[:, j * quarter * vdim : (j + 1) * quarter * vdim],
                probs[j], keys, weight))
    first = sum(pieces[1 : len(pieces) // 2], pieces[0])
    second = sum(pieces[len(pieces) // 2 + 1 :], pieces[len(pieces) // 2])
    latent_grad = key_call(n, first, second)
    weight_grad = finish_call(m, sums)
    return (latent_grad[None], weight_grad)


def solution(mesh):
    return jax.shard_map(
        per_device,
        mesh=mesh,
        in_specs=(
            P("dp", "ctx", None),
            P("dp", "ctx", None, None),
            P("dp", "ctx", None, None),
            P("ctx", None),
            P("dp", None),
            P("dp", None),
            P("dp", "ctx"),
            P("dp", "ctx"),
        ),
        out_specs=(P("dp", "ctx", None), P("ctx", None)),
        check_vma=False,
    )
```

```python
import functools

import jax
import jax.numpy as jnp
from jax import lax
from jax.experimental import pallas as pl
from jax.experimental.pallas import tpu as pltpu
from jax.sharding import PartitionSpec as P

LAT = 512
ROPE = 64
NGROUP = 4
HB = 4
BACK = 3
MESH = pl.DeviceIdType.MESH
VMEM = pltpu.VMEM

score_scale = 192.0 ** (-0.5)
LOG2E = 1.4426950408889634


def enter(targets):
    barrier = pltpu.get_barrier_semaphore()
    for target in targets:
        pl.semaphore_signal(barrier, inc=1, device_id=target, device_id_type=MESH)
    pl.semaphore_wait(barrier, len(targets))


def start_kernel(n, docs, lengths, resumed, latent, groups, reward, keys, bias, weight,
                 mine, got, key_send, key_recv, sum_send, sum_recv):
    me = lax.axis_index("ctx")
    rows = latent.shape[0]
    ids = groups[...]
    gains = reward[...]
    for g in range(NGROUP):
        hit = ids == g
        mine[g : g + 1, :] = jnp.where(hit, gains, 0.0)
        mine[NGROUP + g : NGROUP + g + 1, :] = jnp.where(hit, 1.0, 0.0)
    enter([{"ctx": lax.rem(me + d, n)} for d in range(1, n)])
    sends = []
    for d in range(1, n):
        target = {"ctx": lax.rem(me + d, n)}
        sends.append(pltpu.make_async_remote_copy(
            src_ref=mine, dst_ref=got.at[d - 1], send_sem=sum_send.at[d - 1],
            recv_sem=sum_recv.at[d - 1], device_id=target, device_id_type=MESH))
        sends[-1].start()
    moves = []
    for d in range(1, BACK + 1):
        target = {"ctx": lax.rem(me + d, n)}
        moves.append(pltpu.make_async_remote_copy(
            src_ref=latent, dst_ref=keys.at[pl.ds((BACK - d) * rows, rows)],
            send_sem=key_send.at[d - 1], recv_sem=key_recv.at[d - 1],
            device_id=target, device_id_type=MESH))
        moves[-1].start()
    keys[BACK * rows :, :] = latent[...]
    first = me * rows
    query_pos = first + lax.broadcasted_iota(jnp.int32, (1, rows), 1)
    low = jnp.zeros((1, rows), jnp.int32)
    start = jnp.int32(0)
    before = jnp.int32(0)
    for e in range(docs):
        reach = jnp.where(resumed[0, e] == 1, before, start)
        low = jnp.where(query_pos >= start, reach, low)
        before = start
        start = start + lengths[0, e]
    span = (BACK + 1) * rows
    key_pos = first - BACK * rows + lax.broadcasted_iota(jnp.int32, (span, rows), 0)
    seen = (key_pos >= low) & (key_pos <= query_pos)
    bias[...] = jnp.where(seen, 0.0, -jnp.inf)
    for copy in sends:
        copy.wait()
    total = mine[...]
    for d in range(n - 1):
        total = total + got[d]
    sums = jnp.sum(total, axis=1, keepdims=True)
    mean = jnp.zeros((1, rows), jnp.float32)
    for g in range(NGROUP):
        mean = jnp.where(ids == g, sums[g : g + 1] / sums[NGROUP + g : NGROUP + g + 1], mean)
    token = 0.125 * (gains - mean)
    weight[...] = jnp.transpose(jnp.broadcast_to(token, (rows, rows)))
    for copy in moves:
        copy.wait()


def start_call(n, lengths, resumed, latent, groups, reward):
    rows, width = latent.shape
    span = (BACK + 1) * rows
    vm = pl.BlockSpec(memory_space=VMEM)
    sm = pl.BlockSpec(memory_space=pltpu.SMEM)
    return pl.pallas_call(
        functools.partial(start_kernel, n, lengths.shape[1]),
        out_shape=(
            jax.ShapeDtypeStruct((span, width), jnp.bfloat16),
            jax.ShapeDtypeStruct((span, rows), jnp.float32),
            jax.ShapeDtypeStruct((rows, rows), jnp.float32),
        ),
        in_specs=[sm, sm, vm, vm, vm],
        out_specs=(vm, vm, vm),
        scratch_shapes=[
            VMEM((2 * NGROUP, rows), jnp.float32),
            VMEM((n - 1, 2 * NGROUP, rows), jnp.float32),
            pltpu.SemaphoreType.DMA((BACK,)),
            pltpu.SemaphoreType.DMA((BACK,)),
            pltpu.SemaphoreType.DMA((n - 1,)),
            pltpu.SemaphoreType.DMA((n - 1,)),
        ],
        compiler_params=pltpu.CompilerParams(
            collective_id=0, has_side_effects=True, vmem_limit_bytes=16 << 20),
        cost_estimate=pl.CostEstimate(flops=1 << 20, bytes_accessed=2 << 20, transcendentals=0),
    )(lengths, resumed, latent, groups, reward)


def nt(a, b):
    return lax.dot_general(a, b, (((1,), (1,)), ((), ())), preferred_element_type=jnp.float32)


def nn(a, b):
    return jnp.dot(a, b, preferred_element_type=jnp.float32)


def forward_kernel(with_sum, off, query, grad, keys, values_t, bias, weight, *rest):
    if with_sum:
        partner, prob_ref, away_ref, kept_ref = rest
        middle = away_ref.shape[0]
    else:
        prob_ref, term_ref = rest
    rows = query.shape[2]
    q = jnp.concatenate([query[h] for h in range(HB)], axis=1)
    score = nn(keys[...], q) * (score_scale * LOG2E) + jnp.concatenate([bias[...]] * HB, axis=1)
    peak = jnp.max(score, axis=0, keepdims=True)
    exponent = jnp.exp2(score - peak)
    prob = (exponent * (1.0 / jnp.sum(exponent, axis=0, keepdims=True))).astype(jnp.bfloat16)
    prob_ref[...] = prob
    attended = nn(values_t[...], prob).astype(jnp.bfloat16)
    vdim = grad.shape[2]
    for h in range(HB):
        scaled = (weight[...] * grad[h].astype(jnp.float32)).astype(jnp.bfloat16)
        term = nn(attended[:, h * rows : (h + 1) * rows], scaled)
        part = slice(h * vdim, (h + 1) * vdim)
        if with_sum:
            term = (term + partner[:, part].astype(jnp.float32)).astype(jnp.bfloat16)
            away_ref[:, part] = term[:middle]
            kept_ref[:, part] = term[middle:]
        else:
            term_ref[:, part] = term.astype(jnp.bfloat16)


def forward_call(off, heads, query, grad, keys, values_t, bias, weight, partner=None):
    width, rows = query.shape[1:]
    vdim = grad.shape[2]
    span = keys.shape[0]
    whole = lambda shape: pl.BlockSpec(shape, lambda i, o: (0, 0))
    by_head = lambda shape: pl.BlockSpec(shape, lambda i, o: (o[0] + i, 0, 0))
    column = lambda height, wide: pl.BlockSpec((height, wide), lambda i, o: (0, i))
    in_specs = [
        by_head((HB, width, rows)), by_head((HB, rows, vdim)), whole((span, width)),
        whole((LAT, span)), whole((span, rows)), whole((rows, rows)),
    ]
    args = [query, grad, keys, values_t, bias, weight]
    if partner is not None:
        in_specs.append(column(LAT, HB * vdim))
        args.append(partner)
    terms = 1 if partner is None else 2
    flops = 2 * heads * rows * (span * (width + LAT) + LAT * vdim)
    return pl.pallas_call(
        functools.partial(forward_kernel, partner is not None),
        grid_spec=pltpu.PrefetchScalarGridSpec(
            num_scalar_prefetch=1,
            grid=(heads // HB,),
            in_specs=in_specs,
            out_specs=[column(span, HB * rows)] + [column(LAT // terms, HB * vdim)] * terms,
        ),
        out_shape=[jax.ShapeDtypeStruct((span, heads * rows), jnp.bfloat16)]
        + [jax.ShapeDtypeStruct((LAT // terms, heads * vdim), jnp.bfloat16)] * terms,
        compiler_params=pltpu.CompilerParams(vmem_limit_bytes=48 << 20),
        cost_estimate=pl.CostEstimate(
            flops=flops, bytes_accessed=heads * rows * 4 * (width + span), transcendentals=0),
    )(off, *args)


def backward_kernel(off, query, grad, value_weight, prob_ref, keys, weight, *rest):
    out = rest[-1]
    rows = query.shape[2]
    vdim = grad.shape[2]
    q = jnp.concatenate([query[h] for h in range(HB)], axis=1)
    parts = []
    for h in range(HB):
        scaled = (weight[...] * grad[h].astype(jnp.float32)).astype(jnp.bfloat16)
        parts.append(nt(scaled, value_weight[:, h * vdim : (h + 1) * vdim]).astype(jnp.bfloat16))
    latent_out = jnp.concatenate(parts, axis=0)
    prob_b = prob_ref[...]
    prob = prob_b.astype(jnp.float32)
    prob_grad = nt(keys[:, :LAT], latent_out)
    row_dot = jnp.sum(prob * prob_grad, axis=0, keepdims=True)
    score_grad = (score_scale * prob * (prob_grad - row_dot)).astype(jnp.bfloat16)
    key_part = nt(score_grad, q)
    value_part = nn(prob_b, latent_out)

    @pl.when(pl.program_id(0) == 0)
    def _():
        out[...] = jnp.zeros_like(out)

    out[:, :LAT] += key_part[:, :LAT] + value_part
    out[:, LAT:] += key_part[:, LAT:]


def backward_call(off, shift, heads, query, grad, value_weight, prob, keys, weight, after):
    width, rows = query.shape[1:]
    vdim = grad.shape[2]
    span = keys.shape[0]
    whole = lambda shape: pl.BlockSpec(shape, lambda i, o: (0, 0))
    by_head = lambda shape: pl.BlockSpec(shape, lambda i, o: (o[0] + i, 0, 0))
    column = lambda height, wide: pl.BlockSpec((height, wide), lambda i, o: (0, i))
    flops = 2 * heads * rows * (span * (width + 2 * LAT) + LAT * vdim)
    return pl.pallas_call(
        backward_kernel,
        grid_spec=pltpu.PrefetchScalarGridSpec(
            num_scalar_prefetch=1,
            grid=(heads // HB,),
            in_specs=[
                by_head((HB, width, rows)), by_head((HB, rows, vdim)),
                pl.BlockSpec((LAT, HB * vdim), lambda i, o: (0, shift + i)),
                column(span, HB * rows), whole((span, width)), whole((rows, rows)),
            ] + [pl.BlockSpec(memory_space=pl.ANY)] * len(after),
            out_specs=whole((span, width)),
        ),
        out_shape=jax.ShapeDtypeStruct((span, width), jnp.float32),
        compiler_params=pltpu.CompilerParams(vmem_limit_bytes=48 << 20),
        cost_estimate=pl.CostEstimate(
            flops=flops, bytes_accessed=heads * rows * 4 * (width + span), transcendentals=0),
    )(off, query, grad, value_weight, prob, keys, weight, *after)


def key_kernel(n, first, second, out, term, got, send, recv):
    me = lax.axis_index("ctx")
    rows = out.shape[0]
    term[...] = (first[...] + second[...]).astype(jnp.bfloat16)
    enter([{"ctx": lax.rem(me + d, n)} for d in range(1, BACK + 1)]
          + [{"ctx": lax.rem(me + n - d, n)} for d in range(1, BACK + 1)])
    moves = []
    for d in range(1, BACK + 1):
        moves.append(pltpu.make_async_remote_copy(
            src_ref=term.at[pl.ds((BACK - d) * rows, rows)], dst_ref=got.at[d - 1],
            send_sem=send.at[d - 1], recv_sem=recv.at[d - 1],
            device_id={"ctx": lax.rem(me + n - d, n)}, device_id_type=MESH))
        moves[-1].start()
    total = term[BACK * rows :, :].astype(jnp.float32)
    for d in range(1, BACK + 1):
        moves[d - 1].wait()
        total = total + jnp.where(me + d < n, got[d - 1].astype(jnp.float32), 0.0)
    out[...] = total


def key_call(n, first, second):
    span, width = first.shape
    rows = span // (BACK + 1)
    vm = pl.BlockSpec(memory_space=VMEM)
    return pl.pallas_call(
        functools.partial(key_kernel, n),
        out_shape=jax.ShapeDtypeStruct((rows, width), jnp.float32),
        in_specs=[vm, vm],
        out_specs=vm,
        scratch_shapes=[
            VMEM((span, width), jnp.bfloat16),
            VMEM((BACK, rows, width), jnp.bfloat16),
            pltpu.SemaphoreType.DMA((BACK,)),
            pltpu.SemaphoreType.DMA((BACK,)),
        ],
        compiler_params=pltpu.CompilerParams(
            collective_id=1, has_side_effects=True, vmem_limit_bytes=24 << 20),
        cost_estimate=pl.CostEstimate(flops=1 << 20, bytes_accessed=3 << 20, transcendentals=0),
    )(first, second)


def finish_kernel(m, count, terms, *refs):
    out, across, part, mine, other, x_send, x_recv, c_send, c_recv = refs[count * terms + 1 :]
    parts = []
    for j in range(count):
        total = refs[j * terms][...].astype(jnp.float32)
        for k in range(1, terms):
            total = total + refs[j * terms + k][...].astype(jnp.float32)
        part[j] = total.astype(jnp.bfloat16)
        parts.append(part.at[j])
    me = lax.axis_index("dp")
    core = lax.rem(me, 2)
    chip = me // 2
    chips = m // 2
    wide = part.shape[2]
    half = wide * count
    partner = {"dp": chip * 2 + (1 - core)}
    peers = [{"dp": lax.rem(chip + d, chips) * 2 + core} for d in range(1, chips)]
    enter(peers + [partner])
    moves = []
    for j in range(count):
        row = []
        for d in range(1, chips):
            row.append(pltpu.make_async_remote_copy(
                src_ref=parts[j], dst_ref=across.at[j, chip],
                send_sem=x_send.at[j, d - 1], recv_sem=x_recv.at[j, d - 1],
                device_id=peers[d - 1], device_id_type=MESH))
            row[-1].start()
        moves.append(row)
    swaps = []
    for j in range(count):
        across[j, chip] = parts[j][...]
        for copy in moves[j]:
            copy.wait()
        total = across[j, 0].astype(jnp.float32)
        for k in range(1, chips):
            total = total + across[j, k].astype(jnp.float32)
        rounded = total.astype(jnp.bfloat16)
        mine[j] = rounded
        swaps.append(pltpu.make_async_remote_copy(
            src_ref=mine.at[j], dst_ref=other.at[j], send_sem=c_send.at[j],
            recv_sem=c_recv.at[j], device_id=partner, device_id_type=MESH))
        swaps[-1].start()
        out[:, pl.ds(pl.multiple_of(core * half + j * wide, 128), wide)] = rounded.astype(jnp.float32)
    for j in range(count):
        swaps[j].wait()
        out[:, pl.ds(pl.multiple_of((1 - core) * half + j * wide, 128), wide)] = (
            other[j].astype(jnp.float32))


def finish_call(m, parts, after):
    count = len(parts)
    terms = len(parts[0])
    rows, wide = parts[0][0].shape
    vm = pl.BlockSpec(memory_space=VMEM)
    chips = m // 2
    return pl.pallas_call(
        functools.partial(finish_kernel, m, count, terms),
        out_shape=jax.ShapeDtypeStruct((rows, 2 * wide * count), jnp.float32),
        in_specs=[vm] * (count * terms) + [pl.BlockSpec(memory_space=pl.ANY)],
        out_specs=vm,
        scratch_shapes=[
            VMEM((count, chips, rows, wide), jnp.bfloat16),
            VMEM((count, rows, wide), jnp.bfloat16),
            VMEM((count, rows, wide), jnp.bfloat16),
            VMEM((count, rows, wide), jnp.bfloat16),
            pltpu.SemaphoreType.DMA((count, chips - 1)),
            pltpu.SemaphoreType.DMA((count, chips - 1)),
            pltpu.SemaphoreType.DMA((count,)),
            pltpu.SemaphoreType.DMA((count,)),
        ],
        compiler_params=pltpu.CompilerParams(
            collective_id=2, has_side_effects=True, vmem_limit_bytes=24 << 20),
        cost_estimate=pl.CostEstimate(flops=1 << 20, bytes_accessed=6 << 20, transcendentals=0),
    )(*[term for row in parts for term in row], after)


CHUNKS = 2
LINE = 4
PAIR = 2


def gate_kernel(held, *rest):
    pass


def held_until(held, *after):
    anywhere = pl.BlockSpec(memory_space=pl.ANY)
    return pl.pallas_call(
        gate_kernel,
        out_shape=jax.ShapeDtypeStruct(held.shape, held.dtype),
        in_specs=[anywhere] * (1 + len(after)),
        out_specs=anywhere,
        input_output_aliases={0: 0},
    )(held, *after)


def pair_terms(away, kept, n):
    came = lax.ppermute(away, "ctx", [(i, i ^ 1) for i in range(n)])
    return (kept.astype(jnp.float32) + came.astype(jnp.float32)).astype(jnp.bfloat16)


def line_terms(pair, n):
    rows = pair.shape[0] // LINE
    came = [pair[:rows]]
    for d in range(1, LINE):
        path = [(i, (i // PAIR + d) % LINE * PAIR + i % PAIR) for i in range(n)]
        came.append(lax.ppermute(pair[d * rows : (d + 1) * rows], "ctx", path))
    return came


def in_route_order(values_t, n):
    if n != LINE * PAIR:
        return values_t
    me = lax.axis_index("ctx")
    width, span = values_t.shape
    blocks = values_t.reshape(LINE, PAIR, width // n, span)
    blocks = lax.dynamic_slice_in_dim(
        jnp.concatenate([blocks, blocks], axis=0), me // PAIR, LINE, 0)
    away = lax.dynamic_slice_in_dim(blocks, 1 - me % PAIR, 1, 1)
    kept = lax.dynamic_slice_in_dim(blocks, me % PAIR, 1, 1)
    return jnp.concatenate([away, kept], axis=1).transpose(1, 0, 2, 3).reshape(width, span)


def per_device(latent, query, out_grad, value_weight, doc_lengths, resumed, groups, reward):
    n = lax.axis_size("ctx")
    m = lax.axis_size("dp")
    core = lax.rem(lax.axis_index("dp"), 2)
    heads = query.shape[2]
    half = heads // 2
    quarter = half // CHUNKS
    vdim = out_grad.shape[3]
    swap = [(i, i ^ 1) for i in range(m)]
    keys, bias, weight = start_call(n, doc_lengths, resumed, latent[0], groups, reward)
    half_rows = lax.dynamic_slice_in_dim(value_weight, core * half * vdim, half * vdim, 1)
    half_rows, weight = lax.optimization_barrier((half_rows, weight))
    own_weight = lax.all_gather(half_rows, "ctx", axis=0, tiled=True)
    values_t = in_route_order(keys[:, :LAT].T, n)
    q = jnp.transpose(query[0], (1, 2, 0))
    grad = jnp.transpose(out_grad[0], (1, 0, 2))
    own_at = [((core * half + j * quarter) // HB).astype(jnp.int32).reshape(1) for j in range(CHUNKS)]
    other_at = [(((1 - core) * half + j * quarter) // HB).astype(jnp.int32).reshape(1)
                for j in range(CHUNKS)]
    other_prob, own_prob, arrived, sums = [], [], [], []
    for j in range(CHUNKS):
        prob, term = forward_call(other_at[j], quarter, q, grad, keys, values_t, bias, weight)
        other_prob.append(prob)
        arrived.append(lax.ppermute(term, "dp", swap))
    routed = n == LINE * PAIR
    for j in range(CHUNKS):
        prob, away, kept = forward_call(
            own_at[j], quarter, q, grad, keys, values_t, bias, weight, arrived[j])
        own_prob.append(prob)
        if routed:
            sums.append(pair_terms(away, kept, n))
        else:
            sums.append([lax.psum_scatter(
                jnp.concatenate([away, kept], axis=0), "ctx", scatter_dimension=0, tiled=True)])
    own_weight = held_until(own_weight, own_prob[-1])
    other_weight = lax.ppermute(own_weight, "dp", swap)
    pieces = []
    for at, weights, probs in ((own_at, own_weight, own_prob), (other_at, other_weight, other_prob)):
        for j in range(CHUNKS):
            after = pieces[-1:]
            if routed and weights is own_weight:
                after = after + [sums[j]]
                sums[j] = line_terms(sums[j], n)
            pieces.append(backward_call(
                at[j], j * quarter // HB, quarter, q, grad, weights, probs[j], keys, weight, after))
    first = sum(pieces[1 : len(pieces) // 2], pieces[0])
    second = sum(pieces[len(pieces) // 2 + 1 :], pieces[len(pieces) // 2])
    latent_grad = key_call(n, first, second)
    weight_grad = finish_call(m, sums, latent_grad)
    return (latent_grad[None], weight_grad)


def solution(mesh):
    return jax.shard_map(
        per_device,
        mesh=mesh,
        in_specs=(
            P("dp", "ctx", None),
            P("dp", "ctx", None, None),
            P("dp", "ctx", None, None),
            P("ctx", None),
            P("dp", None),
            P("dp", None),
            P("dp", "ctx"),
            P("dp", "ctx"),
        ),
        out_specs=(P("dp", "ctx", None), P("ctx", None)),
        check_vma=False,
    )
```

```python
import functools

import jax
import jax.numpy as jnp
from jax import lax
from jax.experimental import pallas as pl
from jax.experimental.pallas import tpu as pltpu
from jax.sharding import PartitionSpec as P

LAT = 512
ROPE = 64
NGROUP = 4
HB = 4
BACK = 3
MESH = pl.DeviceIdType.MESH
VMEM = pltpu.VMEM

score_scale = 192.0 ** (-0.5)
LOG2E = 1.4426950408889634


def enter(targets):
    barrier = pltpu.get_barrier_semaphore()
    for target in targets:
        pl.semaphore_signal(barrier, inc=1, device_id=target, device_id_type=MESH)
    pl.semaphore_wait(barrier, len(targets))


def start_kernel(n, docs, lengths, resumed, latent, groups, reward, keys, bias, weight,
                 mine, got, key_send, key_recv, sum_send, sum_recv):
    me = lax.axis_index("ctx")
    rows = latent.shape[0]
    ids = groups[...]
    gains = reward[...]
    for g in range(NGROUP):
        hit = ids == g
        mine[g : g + 1, :] = jnp.where(hit, gains, 0.0)
        mine[NGROUP + g : NGROUP + g + 1, :] = jnp.where(hit, 1.0, 0.0)
    enter([{"ctx": lax.rem(me + d, n)} for d in range(1, n)])
    sends = []
    for d in range(1, n):
        target = {"ctx": lax.rem(me + d, n)}
        sends.append(pltpu.make_async_remote_copy(
            src_ref=mine, dst_ref=got.at[d - 1], send_sem=sum_send.at[d - 1],
            recv_sem=sum_recv.at[d - 1], device_id=target, device_id_type=MESH))
        sends[-1].start()
    moves = []
    for d in range(1, BACK + 1):
        target = {"ctx": lax.rem(me + d, n)}
        moves.append(pltpu.make_async_remote_copy(
            src_ref=latent, dst_ref=keys.at[pl.ds((BACK - d) * rows, rows)],
            send_sem=key_send.at[d - 1], recv_sem=key_recv.at[d - 1],
            device_id=target, device_id_type=MESH))
        pl.when(me + d < n)(moves[-1].start)
    keys[BACK * rows :, :] = latent[...]
    first = me * rows
    query_pos = first + lax.broadcasted_iota(jnp.int32, (1, rows), 1)
    low = jnp.zeros((1, rows), jnp.int32)
    start = jnp.int32(0)
    before = jnp.int32(0)
    for e in range(docs):
        reach = jnp.where(resumed[0, e] == 1, before, start)
        low = jnp.where(query_pos >= start, reach, low)
        before = start
        start = start + lengths[0, e]
    span = (BACK + 1) * rows
    key_pos = first - BACK * rows + lax.broadcasted_iota(jnp.int32, (span, rows), 0)
    seen = (key_pos >= low) & (key_pos <= query_pos)
    bias[...] = jnp.where(seen, 0.0, -jnp.inf)
    for copy in sends:
        copy.wait()
    total = mine[...]
    for d in range(n - 1):
        total = total + got[d]
    sums = jnp.sum(total, axis=1, keepdims=True)
    mean = jnp.zeros((1, rows), jnp.float32)
    for g in range(NGROUP):
        mean = jnp.where(ids == g, sums[g : g + 1] / sums[NGROUP + g : NGROUP + g + 1], mean)
    token = 0.125 * (gains - mean)
    weight[...] = jnp.transpose(jnp.broadcast_to(token, (rows, rows)))
    for d in range(1, BACK + 1):
        pl.when(me + d < n)(moves[d - 1].wait_send)
        pl.when(me >= d)(moves[d - 1].wait_recv)

        @pl.when(me < d)
        def _(d=d):
            keys[(BACK - d) * rows : (BACK + 1 - d) * rows, :] = jnp.zeros_like(latent)


def start_call(n, lengths, resumed, latent, groups, reward):
    rows, width = latent.shape
    span = (BACK + 1) * rows
    vm = pl.BlockSpec(memory_space=VMEM)
    sm = pl.BlockSpec(memory_space=pltpu.SMEM)
    return pl.pallas_call(
        functools.partial(start_kernel, n, lengths.shape[1]),
        out_shape=(
            jax.ShapeDtypeStruct((span, width), jnp.bfloat16),
            jax.ShapeDtypeStruct((span, rows), jnp.float32),
            jax.ShapeDtypeStruct((rows, rows), jnp.float32),
        ),
        in_specs=[sm, sm, vm, vm, vm],
        out_specs=(vm, vm, vm),
        scratch_shapes=[
            VMEM((2 * NGROUP, rows), jnp.float32),
            VMEM((n - 1, 2 * NGROUP, rows), jnp.float32),
            pltpu.SemaphoreType.DMA((BACK,)),
            pltpu.SemaphoreType.DMA((BACK,)),
            pltpu.SemaphoreType.DMA((n - 1,)),
            pltpu.SemaphoreType.DMA((n - 1,)),
        ],
        compiler_params=pltpu.CompilerParams(
            collective_id=0, has_side_effects=True, vmem_limit_bytes=16 << 20),
        cost_estimate=pl.CostEstimate(flops=1 << 20, bytes_accessed=2 << 20, transcendentals=0),
    )(lengths, resumed, latent, groups, reward)


def nt(a, b):
    return lax.dot_general(a, b, (((1,), (1,)), ((), ())), preferred_element_type=jnp.float32)


def nn(a, b):
    return jnp.dot(a, b, preferred_element_type=jnp.float32)


def forward_kernel(with_sum, off, query, grad, keys, values_t, bias, weight, *rest):
    if with_sum:
        partner, prob_ref, term_ref = rest
    else:
        prob_ref, term_ref = rest
    rows = query.shape[2]
    q = jnp.concatenate([query[h] for h in range(HB)], axis=1)
    score = nn(keys[...], q) * (score_scale * LOG2E) + jnp.concatenate([bias[...]] * HB, axis=1)
    peak = jnp.max(score, axis=0, keepdims=True)
    exponent = jnp.exp2(score - peak)
    prob = (exponent * (1.0 / jnp.sum(exponent, axis=0, keepdims=True))).astype(jnp.bfloat16)
    prob_ref[...] = prob
    attended = nn(values_t[...], prob).astype(jnp.bfloat16)
    vdim = grad.shape[2]
    for h in range(HB):
        scaled = (weight[...] * grad[h].astype(jnp.float32)).astype(jnp.bfloat16)
        term = nn(attended[:, h * rows : (h + 1) * rows], scaled)
        part = slice(h * vdim, (h + 1) * vdim)
        if with_sum:
            term = term + partner[:, part].astype(jnp.float32)
        term_ref[:, part] = term.astype(jnp.bfloat16)


def forward_call(off, heads, query, grad, keys, values_t, bias, weight, partner=None):
    width, rows = query.shape[1:]
    vdim = grad.shape[2]
    span = keys.shape[0]
    whole = lambda shape: pl.BlockSpec(shape, lambda i, o: (0, 0))
    by_head = lambda shape: pl.BlockSpec(shape, lambda i, o: (o[0] + i, 0, 0))
    column = lambda height, wide: pl.BlockSpec((height, wide), lambda i, o: (0, i))
    in_specs = [
        by_head((HB, width, rows)), by_head((HB, rows, vdim)), whole((span, width)),
        whole((LAT, span)), whole((span, rows)), whole((rows, rows)),
    ]
    args = [query, grad, keys, values_t, bias, weight]
    if partner is not None:
        in_specs.append(column(LAT, HB * vdim))
        args.append(partner)
    flops = 2 * heads * rows * (span * (width + LAT) + LAT * vdim)
    return pl.pallas_call(
        functools.partial(forward_kernel, partner is not None),
        grid_spec=pltpu.PrefetchScalarGridSpec(
            num_scalar_prefetch=1,
            grid=(heads // HB,),
            in_specs=in_specs,
            out_specs=[column(span, HB * rows), column(LAT, HB * vdim)],
        ),
        out_shape=[
            jax.ShapeDtypeStruct((span, heads * rows), jnp.bfloat16),
            jax.ShapeDtypeStruct((LAT, heads * vdim), jnp.bfloat16),
        ],
        compiler_params=pltpu.CompilerParams(vmem_limit_bytes=48 << 20),
        cost_estimate=pl.CostEstimate(
            flops=flops, bytes_accessed=heads * rows * 4 * (width + span), transcendentals=0),
    )(off, *args)


def backward_kernel(off, query, grad, value_weight, prob_ref, keys, weight, *rest):
    out = rest[-1]
    rows = query.shape[2]
    vdim = grad.shape[2]
    q = jnp.concatenate([query[h] for h in range(HB)], axis=1)
    parts = []
    for h in range(HB):
        scaled = (weight[...] * grad[h].astype(jnp.float32)).astype(jnp.bfloat16)
        parts.append(nt(scaled, value_weight[:, h * vdim : (h + 1) * vdim]).astype(jnp.bfloat16))
    latent_out = jnp.concatenate(parts, axis=0)
    prob_b = prob_ref[...]
    prob = prob_b.astype(jnp.float32)
    prob_grad = nt(keys[:, :LAT], latent_out)
    row_dot = jnp.sum(prob * prob_grad, axis=0, keepdims=True)
    score_grad = (score_scale * prob * (prob_grad - row_dot)).astype(jnp.bfloat16)
    key_part = nt(score_grad, q)
    value_part = nn(prob_b, latent_out)

    @pl.when(pl.program_id(0) == 0)
    def _():
        out[...] = jnp.zeros_like(out)

    out[:, :LAT] += key_part[:, :LAT] + value_part
    out[:, LAT:] += key_part[:, LAT:]


def backward_call(off, heads, query, grad, value_weight, prob, keys, weight, after):
    width, rows = query.shape[1:]
    vdim = grad.shape[2]
    span = keys.shape[0]
    whole = lambda shape: pl.BlockSpec(shape, lambda i, o: (0, 0))
    by_head = lambda shape: pl.BlockSpec(shape, lambda i, o: (o[0] + i, 0, 0))
    column = lambda height, wide: pl.BlockSpec((height, wide), lambda i, o: (0, i))
    flops = 2 * heads * rows * (span * (width + 2 * LAT) + LAT * vdim)
    return pl.pallas_call(
        backward_kernel,
        grid_spec=pltpu.PrefetchScalarGridSpec(
            num_scalar_prefetch=1,
            grid=(heads // HB,),
            in_specs=[
                by_head((HB, width, rows)), by_head((HB, rows, vdim)),
                pl.BlockSpec((LAT, HB * vdim), lambda i, o: (0, o[1] + i)),
                column(span, HB * rows), whole((span, width)), whole((rows, rows)),
            ] + [pl.BlockSpec(memory_space=pl.ANY)] * len(after),
            out_specs=whole((span, width)),
        ),
        out_shape=jax.ShapeDtypeStruct((span, width), jnp.float32),
        compiler_params=pltpu.CompilerParams(vmem_limit_bytes=48 << 20),
        cost_estimate=pl.CostEstimate(
            flops=flops, bytes_accessed=heads * rows * 4 * (width + span), transcendentals=0),
    )(off, query, grad, value_weight, prob, keys, weight, *after)


def key_kernel(n, first, second, out, term, got, send, recv):
    me = lax.axis_index("ctx")
    rows = out.shape[0]
    term[...] = (first[...] + second[...]).astype(jnp.bfloat16)
    enter([{"ctx": lax.rem(me + d, n)} for d in range(1, BACK + 1)]
          + [{"ctx": lax.rem(me + n - d, n)} for d in range(1, BACK + 1)])
    moves = []
    for d in range(1, BACK + 1):
        moves.append(pltpu.make_async_remote_copy(
            src_ref=term.at[pl.ds((BACK - d) * rows, rows)], dst_ref=got.at[d - 1],
            send_sem=send.at[d - 1], recv_sem=recv.at[d - 1],
            device_id={"ctx": lax.rem(me + n - d, n)}, device_id_type=MESH))
        pl.when(me >= d)(moves[-1].start)
    out[...] = term[BACK * rows :, :].astype(jnp.float32)
    for d in range(1, BACK + 1):
        pl.when(me >= d)(moves[d - 1].wait_send)

        @pl.when(me + d < n)
        def _(d=d):
            moves[d - 1].wait_recv()
            out[...] += got[d - 1].astype(jnp.float32)


def key_call(n, first, second):
    span, width = first.shape
    rows = span // (BACK + 1)
    vm = pl.BlockSpec(memory_space=VMEM)
    return pl.pallas_call(
        functools.partial(key_kernel, n),
        out_shape=jax.ShapeDtypeStruct((rows, width), jnp.float32),
        in_specs=[vm, vm],
        out_specs=vm,
        scratch_shapes=[
            VMEM((span, width), jnp.bfloat16),
            VMEM((BACK, rows, width), jnp.bfloat16),
            pltpu.SemaphoreType.DMA((BACK,)),
            pltpu.SemaphoreType.DMA((BACK,)),
        ],
        compiler_params=pltpu.CompilerParams(
            collective_id=1, has_side_effects=True, vmem_limit_bytes=24 << 20),
        cost_estimate=pl.CostEstimate(flops=1 << 20, bytes_accessed=3 << 20, transcendentals=0),
    )(first, second)


def finish_kernel(m, count, terms, *refs):
    out, across, part, mine, other, x_send, x_recv, c_send, c_recv = refs[count * terms + 1 :]
    parts = []
    for j in range(count):
        total = refs[j * terms][...].astype(jnp.float32)
        for k in range(1, terms):
            total = total + refs[j * terms + k][...].astype(jnp.float32)
        part[j] = total.astype(jnp.bfloat16)
        parts.append(part.at[j])
    me = lax.axis_index("dp")
    core = lax.rem(me, 2)
    chip = me // 2
    chips = m // 2
    wide = part.shape[2]
    half = wide * count
    partner = {"dp": chip * 2 + (1 - core)}
    peers = [{"dp": lax.rem(chip + d, chips) * 2 + core} for d in range(1, chips)]
    enter(peers + [partner])
    moves = []
    for j in range(count):
        row = []
        for d in range(1, chips):
            row.append(pltpu.make_async_remote_copy(
                src_ref=parts[j], dst_ref=across.at[j, chip],
                send_sem=x_send.at[j, d - 1], recv_sem=x_recv.at[j, d - 1],
                device_id=peers[d - 1], device_id_type=MESH))
            row[-1].start()
        moves.append(row)
    swaps = []
    for j in range(count):
        across[j, chip] = parts[j][...]
        for copy in moves[j]:
            copy.wait()
        total = across[j, 0].astype(jnp.float32)
        for k in range(1, chips):
            total = total + across[j, k].astype(jnp.float32)
        rounded = total.astype(jnp.bfloat16)
        mine[j] = rounded
        swaps.append(pltpu.make_async_remote_copy(
            src_ref=mine.at[j], dst_ref=other.at[j], send_sem=c_send.at[j],
            recv_sem=c_recv.at[j], device_id=partner, device_id_type=MESH))
        swaps[-1].start()
        out[:, pl.ds(pl.multiple_of(core * half + j * wide, 128), wide)] = rounded.astype(jnp.float32)
    for j in range(count):
        swaps[j].wait()
        out[:, pl.ds(pl.multiple_of((1 - core) * half + j * wide, 128), wide)] = (
            other[j].astype(jnp.float32))


def finish_call(m, parts, after):
    count = len(parts)
    terms = len(parts[0])
    rows, wide = parts[0][0].shape
    vm = pl.BlockSpec(memory_space=VMEM)
    chips = m // 2
    return pl.pallas_call(
        functools.partial(finish_kernel, m, count, terms),
        out_shape=jax.ShapeDtypeStruct((rows, 2 * wide * count), jnp.float32),
        in_specs=[vm] * (count * terms) + [pl.BlockSpec(memory_space=pl.ANY)],
        out_specs=vm,
        scratch_shapes=[
            VMEM((count, chips, rows, wide), jnp.bfloat16),
            VMEM((count, rows, wide), jnp.bfloat16),
            VMEM((count, rows, wide), jnp.bfloat16),
            VMEM((count, rows, wide), jnp.bfloat16),
            pltpu.SemaphoreType.DMA((count, chips - 1)),
            pltpu.SemaphoreType.DMA((count, chips - 1)),
            pltpu.SemaphoreType.DMA((count,)),
            pltpu.SemaphoreType.DMA((count,)),
        ],
        compiler_params=pltpu.CompilerParams(
            collective_id=2, has_side_effects=True, vmem_limit_bytes=24 << 20),
        cost_estimate=pl.CostEstimate(flops=1 << 20, bytes_accessed=6 << 20, transcendentals=0),
    )(*[term for row in parts for term in row], after)


def spread_kernel(terms, *refs):
    out, held, x_send, x_recv, c_send, c_recv = refs[terms + 1 :]
    me = lax.axis_index("dp")
    core = lax.rem(me, 2)
    chip = me // 2
    wide = held.shape[2]
    total = refs[0][...].astype(jnp.float32)
    for k in range(1, terms):
        total = total + refs[k][...].astype(jnp.float32)
    held[0] = total.astype(jnp.bfloat16)
    across = {"dp": (1 - chip) * 2 + core}
    beside = {"dp": chip * 2 + (1 - core)}
    enter([across, beside])

    def move(source, slot, send, recv, target):
        copy = pltpu.make_async_remote_copy(
            src_ref=held.at[source], dst_ref=held.at[slot], send_sem=send, recv_sem=recv,
            device_id=target, device_id_type=MESH)
        copy.start()
        return copy

    def place(slot, at):
        out[:, pl.ds(pl.multiple_of(at * wide, 128), wide)] = held[slot].astype(jnp.float32)

    over = move(0, 1, x_send, x_recv, across)
    near = move(0, 2, c_send.at[0], c_recv.at[0], beside)
    place(0, core * 2 + chip)
    near.wait()
    place(2, (1 - core) * 2 + chip)
    over.wait()
    far = move(1, 3, c_send.at[1], c_recv.at[1], beside)
    place(1, core * 2 + (1 - chip))
    far.wait()
    place(3, (1 - core) * 2 + (1 - chip))


def spread_call(came, after):
    rows, wide = came[0].shape
    vm = pl.BlockSpec(memory_space=VMEM)
    dma = pltpu.SemaphoreType.DMA
    return pl.pallas_call(
        functools.partial(spread_kernel, len(came)),
        out_shape=jax.ShapeDtypeStruct((rows, 4 * wide), jnp.float32),
        in_specs=[vm] * len(came) + [pl.BlockSpec(memory_space=pl.ANY)],
        out_specs=vm,
        scratch_shapes=[VMEM((4, rows, wide), jnp.bfloat16), dma, dma, dma((2,)), dma((2,))],
        compiler_params=pltpu.CompilerParams(
            collective_id=3, has_side_effects=True, vmem_limit_bytes=24 << 20),
        cost_estimate=pl.CostEstimate(flops=1 << 20, bytes_accessed=6 << 20, transcendentals=0),
    )(*came, after)


CHUNKS = 2
LINE = 4
PAIR = 2


def gate_kernel(held, *rest):
    pass


def held_until(held, *after):
    anywhere = pl.BlockSpec(memory_space=pl.ANY)
    return pl.pallas_call(
        gate_kernel,
        out_shape=jax.ShapeDtypeStruct(held.shape, held.dtype),
        in_specs=[anywhere] * (1 + len(after)),
        out_specs=anywhere,
        input_output_aliases={0: 0},
    )(held, *after)


def line_terms(pair, n):
    rows = pair.shape[0] // LINE
    came = [pair[:rows]]
    for d in range(1, LINE):
        path = [(i, (i // PAIR + d) % LINE * PAIR + i % PAIR) for i in range(n)]
        came.append(lax.ppermute(pair[d * rows : (d + 1) * rows], "ctx", path))
    return came


def in_route_order(values_t, n):
    me = lax.axis_index("ctx")
    width, span = values_t.shape
    blocks = values_t.reshape(LINE, PAIR, width // n, span)
    blocks = lax.dynamic_slice_in_dim(
        jnp.concatenate([blocks, blocks], axis=0), me // PAIR, LINE, 0)
    away = lax.dynamic_slice_in_dim(blocks, 1 - me % PAIR, 1, 1)
    kept = lax.dynamic_slice_in_dim(blocks, me % PAIR, 1, 1)
    return jnp.concatenate([away, kept], axis=1).transpose(1, 0, 2, 3).reshape(width, span)


def per_device(latent, query, out_grad, value_weight, doc_lengths, resumed, groups, reward):
    n = lax.axis_size("ctx")
    m = lax.axis_size("dp")
    core = lax.rem(lax.axis_index("dp"), 2)
    heads = query.shape[2]
    half = heads // 2
    quarter = half // CHUNKS
    vdim = out_grad.shape[3]
    swap = [(i, i ^ 1) for i in range(m)]
    keys, bias, weight = start_call(n, doc_lengths, resumed, latent[0], groups, reward)
    half_rows = lax.dynamic_slice_in_dim(value_weight, core * half * vdim, half * vdim, 1)
    half_rows, weight = lax.optimization_barrier((half_rows, weight))
    own_weight = lax.all_gather(half_rows, "ctx", axis=0, tiled=True)
    routed = n == LINE * PAIR and m == 4
    values_t = keys[:, :LAT].T
    if routed:
        values_t = in_route_order(values_t, n)
    q = jnp.transpose(query[0], (1, 2, 0))
    grad = jnp.transpose(out_grad[0], (1, 0, 2))
    chip = lax.axis_index("dp") // 2 if routed else 1
    order = [1 - chip, chip] if routed else list(range(CHUNKS))

    def place(side, part):
        return jnp.asarray((side * half + part * quarter) // HB, jnp.int32).reshape(1)

    own_at = [place(core, part) for part in order]
    other_at = [place(1 - core, part) for part in order]
    other_prob, own_prob, arrived, terms = [], [], [], []
    for j in range(CHUNKS):
        prob, term = forward_call(other_at[j], quarter, q, grad, keys, values_t, bias, weight)
        other_prob.append(prob)
        arrived.append(lax.ppermute(term, "dp", swap))
    for j in range(CHUNKS):
        prob, term = forward_call(
            own_at[j], quarter, q, grad, keys, values_t, bias, weight, arrived[j])
        own_prob.append(prob)
        terms.append(term)
    waits = [[], [], [], []]
    if routed:
        crossed = lax.ppermute(terms[0], "dp", [(i, i ^ 2) for i in range(m)])
        total = terms[1].astype(jnp.float32) + crossed.astype(jnp.float32)
        middle = total.shape[0] // 2
        away = total[:middle].astype(jnp.bfloat16)
        came = lax.ppermute(away, "ctx", [(i, i ^ 1) for i in range(n)])
        pair = (total[middle:] + came.astype(jnp.float32)).astype(jnp.bfloat16)
        lines = line_terms(pair, n)
        waits = [[away], [], [], [pair]]
    else:
        shards = [[lax.psum_scatter(term, "ctx", scatter_dimension=0, tiled=True)] for term in terms]
    own_weight = held_until(own_weight, own_prob[-1])
    other_weight = lax.ppermute(own_weight, "dp", swap)
    pieces = []
    for side, weights, probs in ((core, own_weight, own_prob), (1 - core, other_weight, other_prob)):
        for j in range(CHUNKS):
            at = jnp.concatenate(
                [place(side, order[j]), jnp.asarray(order[j] * quarter // HB, jnp.int32).reshape(1)])
            pieces.append(backward_call(
                at, quarter, q, grad, weights, probs[j], keys, weight,
                pieces[-1:] + waits[len(pieces)]))
    first = pieces[0] + pieces[1]
    second = pieces[2] + pieces[3]
    latent_grad = key_call(n, first, second)
    if routed:
        weight_grad = spread_call(lines, latent_grad)
    else:
        weight_grad = finish_call(m, shards, latent_grad)
    return (latent_grad[None], weight_grad)


def solution(mesh):
    return jax.shard_map(
        per_device,
        mesh=mesh,
        in_specs=(
            P("dp", "ctx", None),
            P("dp", "ctx", None, None),
            P("dp", "ctx", None, None),
            P("ctx", None),
            P("dp", None),
            P("dp", None),
            P("dp", "ctx"),
            P("dp", "ctx"),
        ),
        out_specs=(P("dp", "ctx", None), P("ctx", None)),
        check_vma=False,
    )
```

```python
import functools

import jax
import jax.numpy as jnp
from jax import lax
from jax.experimental import pallas as pl
from jax.experimental.pallas import tpu as pltpu
from jax.sharding import PartitionSpec as P

LAT = 512
ROPE = 64
NGROUP = 4
HB = 4
BACK = 3
MESH = pl.DeviceIdType.MESH
VMEM = pltpu.VMEM

score_scale = 192.0 ** (-0.5)
LOG2E = 1.4426950408889634


def enter(targets):
    barrier = pltpu.get_barrier_semaphore()
    for target in targets:
        pl.semaphore_signal(barrier, inc=1, device_id=target, device_id_type=MESH)
    pl.semaphore_wait(barrier, len(targets))


def start_kernel(n, docs, lengths, resumed, latent, groups, reward, keys, bias, weight,
                 mine, got, key_send, key_recv, sum_send, sum_recv):
    me = lax.axis_index("ctx")
    rows = latent.shape[0]
    ids = groups[...]
    gains = reward[...]
    for g in range(NGROUP):
        hit = ids == g
        mine[g : g + 1, :] = jnp.where(hit, gains, 0.0)
        mine[NGROUP + g : NGROUP + g + 1, :] = jnp.where(hit, 1.0, 0.0)
    enter([{"ctx": lax.rem(me + d, n)} for d in range(1, n)])
    sends = []
    for d in range(1, n):
        target = {"ctx": lax.rem(me + d, n)}
        sends.append(pltpu.make_async_remote_copy(
            src_ref=mine, dst_ref=got.at[d - 1], send_sem=sum_send.at[d - 1],
            recv_sem=sum_recv.at[d - 1], device_id=target, device_id_type=MESH))
        sends[-1].start()
    moves = []
    for d in range(1, BACK + 1):
        target = {"ctx": lax.rem(me + d, n)}
        moves.append(pltpu.make_async_remote_copy(
            src_ref=latent, dst_ref=keys.at[pl.ds((BACK - d) * rows, rows)],
            send_sem=key_send.at[d - 1], recv_sem=key_recv.at[d - 1],
            device_id=target, device_id_type=MESH))
        pl.when(me + d < n)(moves[-1].start)
    keys[BACK * rows :, :] = latent[...]
    first = me * rows
    query_pos = first + lax.broadcasted_iota(jnp.int32, (1, rows), 1)
    low = jnp.zeros((1, rows), jnp.int32)
    start = jnp.int32(0)
    before = jnp.int32(0)
    for e in range(docs):
        reach = jnp.where(resumed[0, e] == 1, before, start)
        low = jnp.where(query_pos >= start, reach, low)
        before = start
        start = start + lengths[0, e]
    span = (BACK + 1) * rows
    key_pos = first - BACK * rows + lax.broadcasted_iota(jnp.int32, (span, rows), 0)
    seen = (key_pos >= low) & (key_pos <= query_pos)
    bias[...] = jnp.where(seen, 0.0, -jnp.inf)
    for copy in sends:
        copy.wait()
    total = mine[...]
    for d in range(n - 1):
        total = total + got[d]
    sums = jnp.sum(total, axis=1, keepdims=True)
    mean = jnp.zeros((1, rows), jnp.float32)
    for g in range(NGROUP):
        mean = jnp.where(ids == g, sums[g : g + 1] / sums[NGROUP + g : NGROUP + g + 1], mean)
    token = 0.125 * (gains - mean)
    weight[...] = jnp.transpose(jnp.broadcast_to(token, (rows, rows)))
    for d in range(1, BACK + 1):
        pl.when(me + d < n)(moves[d - 1].wait_send)
        pl.when(me >= d)(moves[d - 1].wait_recv)

        @pl.when(me < d)
        def _(d=d):
            keys[(BACK - d) * rows : (BACK + 1 - d) * rows, :] = jnp.zeros_like(latent)


def start_call(n, lengths, resumed, latent, groups, reward):
    rows, width = latent.shape
    span = (BACK + 1) * rows
    vm = pl.BlockSpec(memory_space=VMEM)
    sm = pl.BlockSpec(memory_space=pltpu.SMEM)
    return pl.pallas_call(
        functools.partial(start_kernel, n, lengths.shape[1]),
        out_shape=(
            jax.ShapeDtypeStruct((span, width), jnp.bfloat16),
            jax.ShapeDtypeStruct((span, rows), jnp.float32),
            jax.ShapeDtypeStruct((rows, rows), jnp.float32),
        ),
        in_specs=[sm, sm, vm, vm, vm],
        out_specs=(vm, vm, vm),
        scratch_shapes=[
            VMEM((2 * NGROUP, rows), jnp.float32),
            VMEM((n - 1, 2 * NGROUP, rows), jnp.float32),
            pltpu.SemaphoreType.DMA((BACK,)),
            pltpu.SemaphoreType.DMA((BACK,)),
            pltpu.SemaphoreType.DMA((n - 1,)),
            pltpu.SemaphoreType.DMA((n - 1,)),
        ],
        compiler_params=pltpu.CompilerParams(
            collective_id=0, has_side_effects=True, vmem_limit_bytes=16 << 20),
        cost_estimate=pl.CostEstimate(flops=1 << 20, bytes_accessed=2 << 20, transcendentals=0),
    )(lengths, resumed, latent, groups, reward)


def nt(a, b):
    return lax.dot_general(a, b, (((1,), (1,)), ((), ())), preferred_element_type=jnp.float32)


def nn(a, b):
    return jnp.dot(a, b, preferred_element_type=jnp.float32)


def forward_kernel(with_sum, off, query, grad, keys, values_t, bias, weight, *rest):
    if with_sum:
        partner = rest[0]
    prob_ref, term_ref = rest[-2:]
    rows = query.shape[2]
    q = jnp.concatenate([query[h] for h in range(HB)], axis=1)
    score = nn(keys[...], q) * (score_scale * LOG2E) + jnp.concatenate([bias[...]] * HB, axis=1)
    peak = jnp.max(score, axis=0, keepdims=True)
    exponent = jnp.exp2(score - peak)
    prob = (exponent * (1.0 / jnp.sum(exponent, axis=0, keepdims=True))).astype(jnp.bfloat16)
    prob_ref[...] = prob
    attended = nn(values_t[...], prob).astype(jnp.bfloat16)
    vdim = grad.shape[2]
    for h in range(HB):
        scaled = (weight[...] * grad[h].astype(jnp.float32)).astype(jnp.bfloat16)
        term = nn(attended[:, h * rows : (h + 1) * rows], scaled)
        part = slice(h * vdim, (h + 1) * vdim)
        if with_sum:
            term = term + partner[:, part].astype(jnp.float32)
        term_ref[:, part] = term.astype(jnp.bfloat16)


def forward_call(off, heads, query, grad, keys, values_t, bias, weight, partner=None, after=()):
    width, rows = query.shape[1:]
    vdim = grad.shape[2]
    span = keys.shape[0]
    whole = lambda shape: pl.BlockSpec(shape, lambda i, o: (0, 0))
    by_head = lambda shape: pl.BlockSpec(shape, lambda i, o: (o[0] + i, 0, 0))
    column = lambda height, wide: pl.BlockSpec((height, wide), lambda i, o: (0, i))
    in_specs = [
        by_head((HB, width, rows)), by_head((HB, rows, vdim)), whole((span, width)),
        whole((LAT, span)), whole((span, rows)), whole((rows, rows)),
    ]
    args = [query, grad, keys, values_t, bias, weight]
    if partner is not None:
        in_specs.append(column(LAT, HB * vdim))
        args.append(partner)
    in_specs += [pl.BlockSpec(memory_space=pl.ANY)] * len(after)
    args += after
    flops = 2 * heads * rows * (span * (width + LAT) + LAT * vdim)
    return pl.pallas_call(
        functools.partial(forward_kernel, partner is not None),
        grid_spec=pltpu.PrefetchScalarGridSpec(
            num_scalar_prefetch=1,
            grid=(heads // HB,),
            in_specs=in_specs,
            out_specs=[column(span, HB * rows), column(LAT, HB * vdim)],
        ),
        out_shape=[
            jax.ShapeDtypeStruct((span, heads * rows), jnp.bfloat16),
            jax.ShapeDtypeStruct((LAT, heads * vdim), jnp.bfloat16),
        ],
        compiler_params=pltpu.CompilerParams(vmem_limit_bytes=48 << 20),
        cost_estimate=pl.CostEstimate(
            flops=flops, bytes_accessed=heads * rows * 4 * (width + span), transcendentals=0),
    )(off, *args)


def backward_kernel(off, query, grad, value_weight, prob_ref, keys, weight, *rest):
    out = rest[-1]
    rows = query.shape[2]
    vdim = grad.shape[2]
    q = jnp.concatenate([query[h] for h in range(HB)], axis=1)
    parts = []
    for h in range(HB):
        scaled = (weight[...] * grad[h].astype(jnp.float32)).astype(jnp.bfloat16)
        parts.append(nt(scaled, value_weight[:, h * vdim : (h + 1) * vdim]).astype(jnp.bfloat16))
    latent_out = jnp.concatenate(parts, axis=0)
    prob_b = prob_ref[...]
    prob = prob_b.astype(jnp.float32)
    prob_grad = nt(keys[:, :LAT], latent_out)
    row_dot = jnp.sum(prob * prob_grad, axis=0, keepdims=True)
    score_grad = (score_scale * prob * (prob_grad - row_dot)).astype(jnp.bfloat16)
    key_part = nt(score_grad, q)
    value_part = nn(prob_b, latent_out)

    @pl.when(pl.program_id(0) == 0)
    def _():
        out[...] = jnp.zeros_like(out)

    out[:, :LAT] += key_part[:, :LAT] + value_part
    out[:, LAT:] += key_part[:, LAT:]


def backward_call(off, heads, query, grad, value_weight, prob, keys, weight, after):
    width, rows = query.shape[1:]
    vdim = grad.shape[2]
    span = keys.shape[0]
    whole = lambda shape: pl.BlockSpec(shape, lambda i, o: (0, 0))
    by_head = lambda shape: pl.BlockSpec(shape, lambda i, o: (o[0] + i, 0, 0))
    column = lambda height, wide: pl.BlockSpec((height, wide), lambda i, o: (0, i))
    flops = 2 * heads * rows * (span * (width + 2 * LAT) + LAT * vdim)
    return pl.pallas_call(
        backward_kernel,
        grid_spec=pltpu.PrefetchScalarGridSpec(
            num_scalar_prefetch=1,
            grid=(heads // HB,),
            in_specs=[
                by_head((HB, width, rows)), by_head((HB, rows, vdim)),
                pl.BlockSpec((LAT, HB * vdim), lambda i, o: (0, o[1] + i)),
                column(span, HB * rows), whole((span, width)), whole((rows, rows)),
            ] + [pl.BlockSpec(memory_space=pl.ANY)] * len(after),
            out_specs=whole((span, width)),
        ),
        out_shape=jax.ShapeDtypeStruct((span, width), jnp.float32),
        compiler_params=pltpu.CompilerParams(vmem_limit_bytes=48 << 20),
        cost_estimate=pl.CostEstimate(
            flops=flops, bytes_accessed=heads * rows * 4 * (width + span), transcendentals=0),
    )(off, query, grad, value_weight, prob, keys, weight, *after)


def key_kernel(n, first, second, out, term, got, send, recv):
    me = lax.axis_index("ctx")
    rows = out.shape[0]
    term[...] = (first[...] + second[...]).astype(jnp.bfloat16)
    enter([{"ctx": lax.rem(me + d, n)} for d in range(1, BACK + 1)]
          + [{"ctx": lax.rem(me + n - d, n)} for d in range(1, BACK + 1)])
    moves = []
    for d in range(1, BACK + 1):
        moves.append(pltpu.make_async_remote_copy(
            src_ref=term.at[pl.ds((BACK - d) * rows, rows)], dst_ref=got.at[d - 1],
            send_sem=send.at[d - 1], recv_sem=recv.at[d - 1],
            device_id={"ctx": lax.rem(me + n - d, n)}, device_id_type=MESH))
        pl.when(me >= d)(moves[-1].start)
    out[...] = term[BACK * rows :, :].astype(jnp.float32)
    for d in range(1, BACK + 1):
        pl.when(me >= d)(moves[d - 1].wait_send)

        @pl.when(me + d < n)
        def _(d=d):
            moves[d - 1].wait_recv()
            out[...] += got[d - 1].astype(jnp.float32)


def key_call(n, first, second):
    span, width = first.shape
    rows = span // (BACK + 1)
    vm = pl.BlockSpec(memory_space=VMEM)
    return pl.pallas_call(
        functools.partial(key_kernel, n),
        out_shape=jax.ShapeDtypeStruct((rows, width), jnp.float32),
        in_specs=[vm, vm],
        out_specs=vm,
        scratch_shapes=[
            VMEM((span, width), jnp.bfloat16),
            VMEM((BACK, rows, width), jnp.bfloat16),
            pltpu.SemaphoreType.DMA((BACK,)),
            pltpu.SemaphoreType.DMA((BACK,)),
        ],
        compiler_params=pltpu.CompilerParams(
            collective_id=1, has_side_effects=True, vmem_limit_bytes=24 << 20),
        cost_estimate=pl.CostEstimate(flops=1 << 20, bytes_accessed=3 << 20, transcendentals=0),
    )(first, second)


def finish_kernel(m, count, terms, *refs):
    out, across, part, mine, other, x_send, x_recv, c_send, c_recv = refs[count * terms + 1 :]
    parts = []
    for j in range(count):
        total = refs[j * terms][...].astype(jnp.float32)
        for k in range(1, terms):
            total = total + refs[j * terms + k][...].astype(jnp.float32)
        part[j] = total.astype(jnp.bfloat16)
        parts.append(part.at[j])
    me = lax.axis_index("dp")
    core = lax.rem(me, 2)
    chip = me // 2
    chips = m // 2
    wide = part.shape[2]
    half = wide * count
    partner = {"dp": chip * 2 + (1 - core)}
    peers = [{"dp": lax.rem(chip + d, chips) * 2 + core} for d in range(1, chips)]
    enter(peers + [partner])
    moves = []
    for j in range(count):
        row = []
        for d in range(1, chips):
            row.append(pltpu.make_async_remote_copy(
                src_ref=parts[j], dst_ref=across.at[j, chip],
                send_sem=x_send.at[j, d - 1], recv_sem=x_recv.at[j, d - 1],
                device_id=peers[d - 1], device_id_type=MESH))
            row[-1].start()
        moves.append(row)
    swaps = []
    for j in range(count):
        across[j, chip] = parts[j][...]
        for copy in moves[j]:
            copy.wait()
        total = across[j, 0].astype(jnp.float32)
        for k in range(1, chips):
            total = total + across[j, k].astype(jnp.float32)
        rounded = total.astype(jnp.bfloat16)
        mine[j] = rounded
        swaps.append(pltpu.make_async_remote_copy(
            src_ref=mine.at[j], dst_ref=other.at[j], send_sem=c_send.at[j],
            recv_sem=c_recv.at[j], device_id=partner, device_id_type=MESH))
        swaps[-1].start()
        out[:, pl.ds(pl.multiple_of(core * half + j * wide, 128), wide)] = rounded.astype(jnp.float32)
    for j in range(count):
        swaps[j].wait()
        out[:, pl.ds(pl.multiple_of((1 - core) * half + j * wide, 128), wide)] = (
            other[j].astype(jnp.float32))


def finish_call(m, parts, after):
    count = len(parts)
    terms = len(parts[0])
    rows, wide = parts[0][0].shape
    vm = pl.BlockSpec(memory_space=VMEM)
    chips = m // 2
    return pl.pallas_call(
        functools.partial(finish_kernel, m, count, terms),
        out_shape=jax.ShapeDtypeStruct((rows, 2 * wide * count), jnp.float32),
        in_specs=[vm] * (count * terms) + [pl.BlockSpec(memory_space=pl.ANY)],
        out_specs=vm,
        scratch_shapes=[
            VMEM((count, chips, rows, wide), jnp.bfloat16),
            VMEM((count, rows, wide), jnp.bfloat16),
            VMEM((count, rows, wide), jnp.bfloat16),
            VMEM((count, rows, wide), jnp.bfloat16),
            pltpu.SemaphoreType.DMA((count, chips - 1)),
            pltpu.SemaphoreType.DMA((count, chips - 1)),
            pltpu.SemaphoreType.DMA((count,)),
            pltpu.SemaphoreType.DMA((count,)),
        ],
        compiler_params=pltpu.CompilerParams(
            collective_id=2, has_side_effects=True, vmem_limit_bytes=24 << 20),
        cost_estimate=pl.CostEstimate(flops=1 << 20, bytes_accessed=6 << 20, transcendentals=0),
    )(*[term for row in parts for term in row], after)


def spread_kernel(terms, parts, *refs):
    out, held, x_send, x_recv, c_send, c_recv = refs[terms * parts + 1 :]
    me = lax.axis_index("dp")
    core = lax.rem(me, 2)
    chip = me // 2
    wide = held.shape[2]
    slim = wide // parts
    for j in range(parts):
        total = refs[j * terms][...].astype(jnp.float32)
        for k in range(1, terms):
            total = total + refs[j * terms + k][...].astype(jnp.float32)
        held[0, :, j * slim : (j + 1) * slim] = total.astype(jnp.bfloat16)
    across = {"dp": (1 - chip) * 2 + core}
    beside = {"dp": chip * 2 + (1 - core)}
    enter([across, beside])

    def move(source, slot, send, recv, target):
        copy = pltpu.make_async_remote_copy(
            src_ref=held.at[source], dst_ref=held.at[slot], send_sem=send, recv_sem=recv,
            device_id=target, device_id_type=MESH)
        copy.start()
        return copy

    def place(slot, at):
        out[:, pl.ds(pl.multiple_of(at * wide, 128), wide)] = held[slot].astype(jnp.float32)

    over = move(0, 1, x_send, x_recv, across)
    near = move(0, 2, c_send.at[0], c_recv.at[0], beside)
    place(0, core * 2 + chip)
    near.wait()
    place(2, (1 - core) * 2 + chip)
    over.wait()
    far = move(1, 3, c_send.at[1], c_recv.at[1], beside)
    place(1, core * 2 + (1 - chip))
    far.wait()
    place(3, (1 - core) * 2 + (1 - chip))


def spread_call(came, parts, after):
    rows, slim = came[0].shape
    wide = slim * parts
    vm = pl.BlockSpec(memory_space=VMEM)
    dma = pltpu.SemaphoreType.DMA
    return pl.pallas_call(
        functools.partial(spread_kernel, len(came) // parts, parts),
        out_shape=jax.ShapeDtypeStruct((rows, 4 * wide), jnp.float32),
        in_specs=[vm] * len(came) + [pl.BlockSpec(memory_space=pl.ANY)],
        out_specs=vm,
        scratch_shapes=[VMEM((4, rows, wide), jnp.bfloat16), dma, dma, dma((2,)), dma((2,))],
        compiler_params=pltpu.CompilerParams(
            collective_id=3, has_side_effects=True, vmem_limit_bytes=24 << 20),
        cost_estimate=pl.CostEstimate(flops=1 << 20, bytes_accessed=6 << 20, transcendentals=0),
    )(*came, after)


CHUNKS = 2
LINE = 4
PAIR = 2


def gate_kernel(held, *rest):
    pass


def held_until(held, *after):
    anywhere = pl.BlockSpec(memory_space=pl.ANY)
    return pl.pallas_call(
        gate_kernel,
        out_shape=jax.ShapeDtypeStruct(held.shape, held.dtype),
        in_specs=[anywhere] * (1 + len(after)),
        out_specs=anywhere,
        input_output_aliases={0: 0},
    )(held, *after)


def line_terms(pair, n):
    came = [pair[0]]
    for d in range(1, LINE):
        path = [(i, (i // PAIR + d) % LINE * PAIR + i % PAIR) for i in range(n)]
        came.append(lax.ppermute(pair[d], "ctx", path))
    return came


def cross_kernel(term, crossed, *rest):
    away, kept = rest[-2:]
    total = (term[...].astype(jnp.float32) + crossed[...].astype(jnp.float32)).astype(jnp.bfloat16)
    middle = away.shape[0]
    away[...] = total[:middle]
    kept[...] = total[middle:]


def cross_call(term, crossed, part, after):
    rows, wide = crossed.shape
    half = jax.ShapeDtypeStruct((rows // 2, wide), jnp.bfloat16)
    return pl.pallas_call(
        cross_kernel,
        grid=(1,),
        out_shape=[half, half],
        in_specs=[
            pl.BlockSpec((rows, wide), lambda i: (0, part)),
            pl.BlockSpec((rows, wide), lambda i: (0, 0)),
        ] + [pl.BlockSpec(memory_space=pl.ANY)] * len(after),
        out_specs=[pl.BlockSpec((rows // 2, wide), lambda i: (0, 0))] * 2,
        compiler_params=pltpu.CompilerParams(vmem_limit_bytes=24 << 20),
    )(term, crossed, *after)


def pair_kernel(kept, came, after, *outs):
    total = (kept[...].astype(jnp.float32) + came[...].astype(jnp.float32)).astype(jnp.bfloat16)
    rows = outs[0].shape[0]
    for d in range(LINE):
        outs[d][...] = total[d * rows : (d + 1) * rows]


def pair_call(kept, came, after):
    rows, wide = kept.shape
    block = lambda height: pl.BlockSpec((height, wide), lambda i: (0, 0))
    return pl.pallas_call(
        pair_kernel,
        grid=(1,),
        out_shape=[jax.ShapeDtypeStruct((rows // LINE, wide), jnp.bfloat16)] * LINE,
        in_specs=[block(rows), block(rows), pl.BlockSpec(memory_space=pl.ANY)],
        out_specs=[block(rows // LINE)] * LINE,
        compiler_params=pltpu.CompilerParams(vmem_limit_bytes=24 << 20),
    )(kept, came, after)


def in_route_order(values_t, n):
    me = lax.axis_index("ctx")
    width, span = values_t.shape
    blocks = values_t.reshape(LINE, PAIR, width // n, span)
    blocks = lax.dynamic_slice_in_dim(
        jnp.concatenate([blocks, blocks], axis=0), me // PAIR, LINE, 0)
    away = lax.dynamic_slice_in_dim(blocks, 1 - me % PAIR, 1, 1)
    kept = lax.dynamic_slice_in_dim(blocks, me % PAIR, 1, 1)
    return jnp.concatenate([away, kept], axis=1).transpose(1, 0, 2, 3).reshape(width, span)


def per_device(latent, query, out_grad, value_weight, doc_lengths, resumed, groups, reward):
    n = lax.axis_size("ctx")
    m = lax.axis_size("dp")
    core = lax.rem(lax.axis_index("dp"), 2)
    heads = query.shape[2]
    half = heads // 2
    quarter = half // CHUNKS
    vdim = out_grad.shape[3]
    swap = [(i, i ^ 1) for i in range(m)]
    keys, bias, weight = start_call(n, doc_lengths, resumed, latent[0], groups, reward)
    half_rows = lax.dynamic_slice_in_dim(value_weight, core * half * vdim, half * vdim, 1)
    half_rows, weight = lax.optimization_barrier((half_rows, weight))
    own_weight = lax.all_gather(half_rows, "ctx", axis=0, tiled=True)
    routed = n == LINE * PAIR and m == 4
    values_t = keys[:, :LAT].T
    if routed:
        values_t = in_route_order(values_t, n)
    q = jnp.transpose(query[0], (1, 2, 0))
    grad = jnp.transpose(out_grad[0], (1, 0, 2))
    chip = lax.axis_index("dp") // 2 if routed else 1
    order = [1 - chip, chip] if routed else list(range(CHUNKS))

    def place(side, part):
        return jnp.asarray((side * half + part * quarter) // HB, jnp.int32).reshape(1)

    own_at = [place(core, part) for part in order]
    other_at = [place(1 - core, part) for part in order]
    other_prob, own_prob, arrived, terms = [], [], [], []
    for j in range(CHUNKS):
        prob, term = forward_call(other_at[j], quarter, q, grad, keys, values_t, bias, weight)
        other_prob.append(prob)
        arrived.append(lax.ppermute(term, "dp", swap))
    for j in range(CHUNKS):
        prob, term = forward_call(
            own_at[j], quarter, q, grad, keys, values_t, bias, weight, arrived[j], own_prob[:])
        own_prob.append(prob)
        terms.append(term)
    if routed:
        wide = terms[0].shape[1] // 2
        crossed = [lax.ppermute(
            terms[0][:, part * wide : (part + 1) * wide], "dp", [(i, i ^ 2) for i in range(m)])
            for part in range(2)]
        kepts, cames = [], []
    else:
        shards = [[lax.psum_scatter(term, "ctx", scatter_dimension=0, tiled=True)] for term in terms]
    own_weight = held_until(own_weight, *own_prob)
    other_weight = lax.ppermute(own_weight, "dp", swap)
    pieces, lines = [], []
    for side, weights, probs in ((core, own_weight, own_prob), (1 - core, other_weight, other_prob)):
        for j in range(CHUNKS):
            at = jnp.concatenate(
                [place(side, order[j]), jnp.asarray(order[j] * quarter // HB, jnp.int32).reshape(1)])
            after = pieces[-1:]
            if routed and len(pieces) < 2:
                part = len(pieces)
                away, kept = cross_call(terms[1], crossed[part], part, pieces[-1:])
                kepts.append(kept)
                cames.append(lax.ppermute(away, "ctx", [(i, i ^ 1) for i in range(n)]))
                after = after + [away]
            if routed and 1 <= len(pieces) <= 2:
                pair = pair_call(kepts[len(pieces) - 1], cames[len(pieces) - 1], pieces[-1])
                lines = lines + line_terms(pair, n)
                after = after + [pair[0]]
            pieces.append(backward_call(
                at, quarter, q, grad, weights, probs[j], keys, weight, after))
    first = pieces[0] + pieces[1]
    second = pieces[2] + pieces[3]
    latent_grad = key_call(n, first, second)
    if routed:
        weight_grad = spread_call(lines, 2, latent_grad)
    else:
        weight_grad = finish_call(m, shards, latent_grad)
    return (latent_grad[None], weight_grad)


def solution(mesh):
    return jax.shard_map(
        per_device,
        mesh=mesh,
        in_specs=(
            P("dp", "ctx", None),
            P("dp", "ctx", None, None),
            P("dp", "ctx", None, None),
            P("ctx", None),
            P("dp", None),
            P("dp", None),
            P("dp", "ctx"),
            P("dp", "ctx"),
        ),
        out_specs=(P("dp", "ctx", None), P("ctx", None)),
        check_vma=False,
    )
```
